256 devices in a mesh: inner: 16 (over x_hi, z), outer: 8 (over x_lo, y), head: 2 (over core).
Axes of the slice: x: 4 (x_hi: 2, x_lo: 2; x = x_hi * 2 + x_lo), y: 4, z: 8, core: 2. Of those that a mesh axis runs over, the one named last changes fastest.
Arguments:
- query_rows: bfloat16 [32768, 2560], P(('inner', 'outer', 'head')), may hold values from -10 to 10
- key_rows: bfloat16 [32768, 2560], P(('inner', 'outer', 'head')), may hold values from -4 to 4
- value_rows: bfloat16 [32768, 2560], P(('inner', 'outer', 'head')), may hold values from -6 to 6
Outputs:
- attended: bfloat16 [32768, 2560], P(('inner', 'outer', 'head'))
The draws below stay inside these ranges and needn't reach their ends.
All inputs are finite; a program needn't handle non-finite values.
Results may differ from the reference program's by a relative error of at most 0.0054.
Values may be sent and summed in bfloat16 or wider, within the bound.
A program may use at most 64 MiB of HBM per device.

```python
import math
import jax
import jax.numpy as jnp
from jax import lax

H = 20
HD = 128
ISTEPS = 2
OSTEPS = 2
ROWS = 256
SEQ = 32768
N_INNER = 16
N_OUTER = 8


def draw_query_rows(key, part):
    key = jax.random.fold_in(key, 11)
    result = 2.5 * jax.random.truncated_normal(key, -4.0, 4.0, (SEQ, H * HD), jnp.float32)
    return result.astype(jnp.bfloat16)


def draw_key_rows(key, part):
    key = jax.random.fold_in(key, 23)
    result = jax.random.truncated_normal(key, -4.0, 4.0, (SEQ, H * HD), jnp.float32)
    return result.astype(jnp.bfloat16)


def level_of(own_key, shape, split, smallest, largest):
    def one(axis_at, parts):
        steps = jax.random.uniform(jax.random.fold_in(jax.random.fold_in(own_key, 6), axis_at), (parts,), jnp.float32, smallest / len(split), largest / len(split))
        return jnp.repeat(jnp.exp(steps), shape[axis_at] // parts).reshape((-1,) + (1,) * (len(shape) - axis_at - 1))

    factor_of = one(*split[0])
    for cut in split[1:]:
        factor_of = factor_of * one(*cut)
    return factor_of


def normal_values(rng, dims, deviation, reach, split=(), held_as=jnp.bfloat16):
    loudness = level_of(rng, dims, split, -0.22, 0.18) if split else 1.0
    entries = jax.random.normal(rng, dims, jnp.float32) * deviation * loudness
    return jnp.minimum(jnp.maximum(entries, -reach), reach).astype(held_as)


def setup_inputs(seed: int = 0) -> dict:
    keys = jax.random.split(jax.random.key(seed), 4)
    query_rows = draw_query_rows(jax.random.fold_in(keys[3], 71), 0)
    key_rows = draw_key_rows(jax.random.fold_in(keys[3], 71), 0)
    value_rows = normal_values(keys[2], (SEQ, H * HD), 1.0, 6.0, ((0, 256),))
    return dict(query_rows=query_rows, key_rows=key_rows, value_rows=value_rows)


def reference(query_rows, key_rows, value_rows):
    columns = H * HD

    def one_block(position):
        inner_pos = position // N_OUTER
        outer_pos = position % N_OUTER
        start = (position * ROWS).astype(jnp.int32)
        query_heads = lax.dynamic_slice_in_dim(query_rows, start, ROWS, 0).astype(jnp.float32).reshape(ROWS, H, HD)
        key_parts = []
        value_parts = []
        for outer_step in range(OSTEPS):
            for inner_step in range(ISTEPS):
                source = (inner_pos - inner_step) % N_INNER * N_OUTER + (outer_pos - outer_step) % N_OUTER
                begin = (source * ROWS).astype(jnp.int32)
                key_parts.append(lax.dynamic_slice_in_dim(key_rows, begin, ROWS, 0))
                value_parts.append(lax.dynamic_slice_in_dim(value_rows, begin, ROWS, 0))
        window_keys = jnp.concatenate(key_parts, 0).astype(jnp.float32).reshape(-1, H, HD)
        window_values = jnp.concatenate(value_parts, 0).astype(jnp.float32).reshape(-1, H, HD)
        scores = jnp.einsum('qhd,khd->qhk', query_heads, window_keys) / math.sqrt(HD)
        row_max = lax.optimization_barrier(jnp.max(scores, axis=2, keepdims=True))
        exponent = jnp.exp(scores - row_max)
        weight_sum = lax.optimization_barrier(jnp.sum(exponent, axis=2))
        weights = lax.optimization_barrier(exponent.astype(jnp.bfloat16)).astype(jnp.float32)
        numerator = jnp.einsum('qhk,khd->qhd', weights, window_values)
        return (numerator / weight_sum[:, :, None]).reshape(ROWS, columns).astype(jnp.bfloat16)
    blocks = lax.map(one_block, jnp.arange(N_INNER * N_OUTER, dtype=jnp.int32))
    return blocks.reshape(N_INNER * N_OUTER * ROWS, columns)
```

```python
import functools
import math

import jax
import jax.numpy as jnp
from jax import lax
from jax.experimental import pallas as pl
from jax.experimental.pallas import tpu as pltpu
from jax.sharding import PartitionSpec as P

HD = 128
MESH = pl.DeviceIdType.MESH
LANE = 128
TAIL = 16
LAG = 2


def cols(at, count=1):
    return pl.ds(pl.multiple_of(at * HD, HD), count * HD)


def halves(at):
    return pl.ds(pl.multiple_of(at * LANE, LANE), LANE)


def split_sum(x):
    high = x.astype(jnp.bfloat16)
    rest = x - high.astype(jnp.float32)
    mid = rest.astype(jnp.bfloat16)
    low = (rest - mid.astype(jnp.float32)).astype(jnp.bfloat16)
    row = lax.broadcasted_iota(jnp.int32, (TAIL, x.shape[1]), 0)
    wide = [jnp.broadcast_to(part.astype(jnp.float32), (TAIL, x.shape[1])) for part in (high, mid, low)]
    tile = jnp.where(row == 0, wide[0], jnp.where(row == 1, wide[1], jnp.where(row == 2, wide[2], 0.0)))
    return tile.astype(jnp.bfloat16)


def kernel(
    n_inner, n_outer, heads,
    q_hbm, k_hbm, v_hbm, o_hbm,
    q_all, kv_own, kv_far, o_out, o_mine, part_own, part_far, result,
    own_sem, swap_send, swap_recv, q_send, q_recv, kv_send, kv_recv,
    far_send, far_recv, mine_send, mine_recv, out_sem,
):
    inner, outer, core = lax.axis_index("inner"), lax.axis_index("outer"), lax.axis_index("head")
    rows = q_hbm.shape[0]
    other = 1 - core
    inner_up, inner_down = lax.rem(inner + 1, n_inner), lax.rem(inner + n_inner - 1, n_inner)
    outer_up, outer_down = lax.rem(outer + 1, n_outer), lax.rem(outer + n_outer - 1, n_outer)
    my_rows = pl.ds(pl.multiple_of(core * rows, rows), rows)

    own = []
    for at, (src, dst) in enumerate(((q_hbm, q_all.at[0]), (k_hbm, kv_own.at[0]), (v_hbm, kv_own.at[1]))):
        copy = pltpu.make_async_copy(src.at[:, cols(core * heads, heads)], dst.at[my_rows, :], own_sem.at[at])
        copy.start()
        own.append(copy)

    barrier = pltpu.get_barrier_semaphore()
    greeted = [(inner, outer, other)]
    for c in range(2):
        greeted += [(inner_up, outer, c), (inner_down, outer, c), (inner, outer_up, c), (inner, outer_down, c)]
    for device in greeted:
        pl.semaphore_signal(barrier, inc=1, device_id=device, device_id_type=MESH)
    pl.semaphore_wait(barrier, len(greeted))

    swaps = []
    for at, (src, dst) in enumerate(((q_hbm, q_all.at[0]), (k_hbm, kv_own.at[0]), (v_hbm, kv_own.at[1]))):
        copy = pltpu.make_async_remote_copy(
            src_ref=src.at[:, cols(other * heads, heads)], dst_ref=dst.at[my_rows, :],
            send_sem=swap_send.at[at], recv_sem=swap_recv.at[at],
            device_id=(inner, outer, other), device_id_type=MESH,
        )
        copy.start()
        swaps.append(copy)

    def send_head(j, _):
        for c in range(2):
            pltpu.make_async_remote_copy(
                src_ref=q_hbm.at[:, cols(c * heads + j)], dst_ref=q_all.at[1, my_rows, cols(j)],
                send_sem=q_send, recv_sem=q_recv.at[j],
                device_id=(inner_down, outer, c), device_id_type=MESH,
            ).start()
        for at, src in enumerate((k_hbm, v_hbm)):
            for c in range(2):
                pltpu.make_async_remote_copy(
                    src_ref=src.at[:, cols(c * heads + j)], dst_ref=kv_far.at[at, my_rows, cols(j)],
                    send_sem=kv_send.at[at], recv_sem=kv_recv.at[j],
                    device_id=(inner, outer_up, c), device_id_type=MESH,
                ).start()
        return 0

    lax.fori_loop(0, heads, send_head, 0)

    for copy in own:
        copy.wait()
    for copy in swaps:
        copy.wait()

    factor = math.log2(math.e) / math.sqrt(HD)

    def attend(q, j):
        keys = (kv_own[0, :, cols(j)], kv_far[0, :, cols(j)])
        values = (kv_own[1, :, cols(j)], kv_far[1, :, cols(j)])
        scores = [
            lax.dot_general(k, q, (((1,), (1,)), ((), ())), preferred_element_type=jnp.float32) for k in keys
        ]
        top = jnp.max(jnp.maximum(scores[0], scores[1]), axis=0, keepdims=True)
        weights = [jnp.exp2((s - top) * factor) for s in scores]
        total = jnp.sum(weights[0] + weights[1], axis=0, keepdims=True)
        summed = sum(
            lax.dot_general(
                v, w.astype(jnp.bfloat16), (((0,), (0,)), ((), ())), preferred_element_type=jnp.float32
            )
            for v, w in zip(values, weights)
        )
        return (summed * (1.0 / total)).astype(jnp.bfloat16), split_sum(top * factor + jnp.log2(total))

    def merge(j):
        for c in range(2):
            g = c * heads + j
            pltpu.make_async_copy(part_far.at[g], part_far.at[g], far_recv.at[g]).wait()

        pltpu.make_async_copy(
            part_own.at[other * heads + j], part_own.at[other * heads + j], mine_recv.at[j]
        ).wait()
        for c in range(2):
            g = c * heads + j
            logs = []
            for part in (part_own, part_far):
                tile = part[g, HD:, :].astype(jnp.float32)
                logs.append(tile[0:1] + tile[1:2] + tile[2:3])
            share_own = 1.0 / (1.0 + jnp.exp2(logs[1] - logs[0]))
            share_far = 1.0 / (1.0 + jnp.exp2(logs[0] - logs[1]))
            mixed = (
                part_own[g, :HD, :].astype(jnp.float32) * share_own
                + part_far[g, :HD, :].astype(jnp.float32) * share_far
            )
            result[:, cols(g)] = mixed.T.astype(jnp.bfloat16)
            pltpu.make_async_copy(result.at[:, cols(g)], o_hbm.at[:, cols(g)], out_sem).start()

    def head_step(j, _):
        pltpu.make_async_copy(q_all.at[1, :, cols(j)], q_all.at[1, :, cols(j)], q_recv.at[j]).wait()
        pltpu.make_async_copy(kv_far.at[:, :, cols(j)], kv_far.at[:, :, cols(j)], kv_recv.at[j]).wait()
        g = core * heads + j
        block, logs = attend(q_all[1, :, cols(j)], j)
        o_out[j, :HD, :] = block
        o_out[j, HD:, :] = logs
        for c in range(2):
            pltpu.make_async_remote_copy(
                src_ref=o_out.at[j, :, halves(c)], dst_ref=part_far.at[g],
                send_sem=far_send, recv_sem=far_recv.at[g],
                device_id=(inner_up, outer, c), device_id_type=MESH,
            ).start()
        block, logs = attend(q_all[0, :, cols(j)], j)
        o_mine[j, :HD, :] = block
        o_mine[j, HD:, :] = logs
        pltpu.make_async_remote_copy(
            src_ref=o_mine.at[j, :, halves(other)], dst_ref=part_own.at[g],
            send_sem=mine_send, recv_sem=mine_recv.at[j],
            device_id=(inner, outer, other), device_id_type=MESH,
        ).start()
        part_own[g] = o_mine[j, :, halves(core)]

        @pl.when(j >= LAG)
        def _():
            merge(j - LAG)

        return 0

    lax.fori_loop(0, heads, head_step, 0)
    for j in range(heads - LAG, heads):
        merge(j)

    pltpu.make_async_copy(result, o_hbm, out_sem).wait()
    pltpu.make_async_copy(q_hbm, q_hbm, q_send).wait()
    pltpu.make_async_copy(k_hbm, k_hbm, kv_send.at[0]).wait()
    pltpu.make_async_copy(v_hbm, v_hbm, kv_send.at[1]).wait()
    pltpu.make_async_copy(o_out, o_out, far_send).wait()
    pltpu.make_async_copy(o_mine.at[:, :, halves(0)], o_mine.at[:, :, halves(0)], mine_send).wait()


def solution(mesh):
    n_inner, n_outer = mesh.shape["inner"], mesh.shape["outer"]

    def per_device(q, k, v):
        rows, width = q.shape
        heads = width // HD // 2
        both = 2 * rows
        dma = pltpu.SemaphoreType.DMA
        return pl.pallas_call(
            functools.partial(kernel, n_inner, n_outer, heads),
            out_shape=jax.ShapeDtypeStruct((rows, width), jnp.bfloat16),
            in_specs=[pl.BlockSpec(memory_space=pl.ANY)] * 3,
            out_specs=pl.BlockSpec(memory_space=pl.ANY),
            scratch_shapes=[
                pltpu.VMEM((2, both, width // 2), jnp.bfloat16),
                pltpu.VMEM((2, both, width // 2), jnp.bfloat16),
                pltpu.VMEM((2, both, width // 2), jnp.bfloat16),
                pltpu.VMEM((heads, HD + TAIL, both), jnp.bfloat16),
                pltpu.VMEM((heads, HD + TAIL, both), jnp.bfloat16),
                pltpu.VMEM((2 * heads, HD + TAIL, rows), jnp.bfloat16),
                pltpu.VMEM((2 * heads, HD + TAIL, rows), jnp.bfloat16),
                pltpu.VMEM((rows, width), jnp.bfloat16),
                dma((3,)), dma((3,)), dma((3,)),
                dma, dma((heads,)), dma((2,)), dma((heads,)),
                dma, dma((2 * heads,)), dma, dma((heads,)), dma,
            ],
            compiler_params=pltpu.CompilerParams(
                collective_id=0, has_side_effects=True, vmem_limit_bytes=32 << 20
            ),
        )(q, k, v)

    spec = P(("inner", "outer", "head"), None)
    return jax.shard_map(per_device, mesh=mesh, in_specs=(spec,) * 3, out_specs=spec, check_vma=False)
```

```python
import functools
import math

import jax
import jax.numpy as jnp
from jax import lax
from jax.experimental import pallas as pl
from jax.experimental.pallas import tpu as pltpu
from jax.sharding import PartitionSpec as P

HD = 128
MESH = pl.DeviceIdType.MESH
LANE = 128
TAIL = 16
LAG = 2


def cols(at, count=1):
    return pl.ds(pl.multiple_of(at * HD, HD), count * HD)


def halves(at):
    return pl.ds(pl.multiple_of(at * LANE, LANE), LANE)


def split_sum(x):
    high = x.astype(jnp.bfloat16)
    rest = x - high.astype(jnp.float32)
    mid = rest.astype(jnp.bfloat16)
    low = (rest - mid.astype(jnp.float32)).astype(jnp.bfloat16)
    row = lax.broadcasted_iota(jnp.int32, (TAIL, x.shape[1]), 0)
    wide = [jnp.broadcast_to(part.astype(jnp.float32), (TAIL, x.shape[1])) for part in (high, mid, low)]
    tile = jnp.where(row == 0, wide[0], jnp.where(row == 1, wide[1], jnp.where(row == 2, wide[2], 0.0)))
    return tile.astype(jnp.bfloat16)


def kernel(
    n_inner, n_outer, heads,
    q_hbm, k_hbm, v_hbm, o_hbm,
    q_all, kv_own, kv_in, o_out, o_mine, part_own, part_far, result,
    own_sem, swap_send, swap_recv, q_send, q_recv, kv_send, kv_recv, pass_send,
    far_send, far_recv, mine_send, mine_recv, out_sem,
):
    inner, outer, core = lax.axis_index("inner"), lax.axis_index("outer"), lax.axis_index("head")
    rows = q_hbm.shape[0]
    other = 1 - core
    inner_up, inner_down = lax.rem(inner + 1, n_inner), lax.rem(inner + n_inner - 1, n_inner)
    outer_up, outer_down = lax.rem(outer + 1, n_outer), lax.rem(outer + n_outer - 1, n_outer)
    along = n_outer // 2
    side, y = outer // along, lax.rem(outer, along)
    flipped = (1 - side) * along + y
    ring_up, ring_down = side * along + lax.rem(y + 1, along), side * along + lax.rem(y + along - 1, along)
    kv_far = kv_in.at[0]
    my_rows = pl.ds(pl.multiple_of(core * rows, rows), rows)

    own = []
    for at, (src, dst) in enumerate(((q_hbm, q_all.at[0]), (k_hbm, kv_own.at[0]), (v_hbm, kv_own.at[1]))):
        copy = pltpu.make_async_copy(src.at[:, cols(core * heads, heads)], dst.at[my_rows, :], own_sem.at[at])
        copy.start()
        own.append(copy)

    barrier = pltpu.get_barrier_semaphore()
    greeted = [(inner, outer, other)]
    for c in range(2):
        greeted += [(inner_up, outer, c), (inner_down, outer, c), (inner, outer_up, c), (inner, outer_down, c)]
        greeted += [(inner, ring_up, c), (inner, ring_down, c), (inner, flipped, c)]
    for device in greeted:
        pl.semaphore_signal(barrier, inc=1, device_id=device, device_id_type=MESH)
    pl.semaphore_wait(barrier, len(greeted))

    swaps = []
    for at, (src, dst) in enumerate(((q_hbm, q_all.at[0]), (k_hbm, kv_own.at[0]), (v_hbm, kv_own.at[1]))):
        copy = pltpu.make_async_remote_copy(
            src_ref=src.at[:, cols(other * heads, heads)], dst_ref=dst.at[my_rows, :],
            send_sem=swap_send.at[at], recv_sem=swap_recv.at[at],
            device_id=(inner, outer, other), device_id_type=MESH,
        )
        copy.start()
        swaps.append(copy)

    def send_head(j, _):
        for c in range(2):
            pltpu.make_async_remote_copy(
                src_ref=q_hbm.at[:, cols(c * heads + j)], dst_ref=q_all.at[1, my_rows, cols(j)],
                send_sem=q_send, recv_sem=q_recv.at[j],
                device_id=(inner_down, outer, c), device_id_type=MESH,
            ).start()
        by_ring = jnp.where((y == along - 1) & (lax.rem(j, 2) == 0), 1, 0)
        target = jnp.where(by_ring == 1, ring_up, outer_up)
        for at, src in enumerate((k_hbm, v_hbm)):
            for c in range(2):
                pltpu.make_async_remote_copy(
                    src_ref=src.at[:, cols(c * heads + j)], dst_ref=kv_in.at[by_ring, at, my_rows, cols(j)],
                    send_sem=kv_send.at[at], recv_sem=kv_recv.at[by_ring, j],
                    device_id=(inner, target, c), device_id_type=MESH,
                ).start()
        return 0

    lax.fori_loop(0, heads, send_head, 0)

    for copy in own:
        copy.wait()
    for copy in swaps:
        copy.wait()

    factor = math.log2(math.e) / math.sqrt(HD)

    def attend(q, j):
        keys = (kv_own[0, :, cols(j)], kv_in[0, 0, :, cols(j)])
        values = (kv_own[1, :, cols(j)], kv_in[0, 1, :, cols(j)])
        scores = [
            lax.dot_general(k, q, (((1,), (1,)), ((), ())), preferred_element_type=jnp.float32) for k in keys
        ]
        top = jnp.max(jnp.maximum(scores[0], scores[1]), axis=0, keepdims=True)
        weights = [jnp.exp2((s - top) * factor) for s in scores]
        total = jnp.sum(weights[0] + weights[1], axis=0, keepdims=True)
        summed = sum(
            lax.dot_general(
                v, w.astype(jnp.bfloat16), (((0,), (0,)), ((), ())), preferred_element_type=jnp.float32
            )
            for v, w in zip(values, weights)
        )
        return (summed * (1.0 / total)).astype(jnp.bfloat16), split_sum(top * factor + jnp.log2(total))

    def merge(j):
        for c in range(2):
            g = c * heads + j
            pltpu.make_async_copy(part_far.at[g], part_far.at[g], far_recv.at[g]).wait()

        pltpu.make_async_copy(
            part_own.at[other * heads + j], part_own.at[other * heads + j], mine_recv.at[j]
        ).wait()
        for c in range(2):
            g = c * heads + j
            logs = []
            for part in (part_own, part_far):
                tile = part[g, HD:, :].astype(jnp.float32)
                logs.append(tile[0:1] + tile[1:2] + tile[2:3])
            share_own = 1.0 / (1.0 + jnp.exp2(logs[1] - logs[0]))
            share_far = 1.0 / (1.0 + jnp.exp2(logs[0] - logs[1]))
            mixed = (
                part_own[g, :HD, :].astype(jnp.float32) * share_own
                + part_far[g, :HD, :].astype(jnp.float32) * share_far
            )
            result[:, cols(g)] = mixed.T.astype(jnp.bfloat16)
            pltpu.make_async_copy(result.at[:, cols(g)], o_hbm.at[:, cols(g)], out_sem).start()

    def head_step(j, _):
        @pl.when((y == 0) & (lax.rem(j, 2) == 0))
        def _():
            passing = kv_in.at[1, :, :, cols(j)]
            pltpu.make_async_copy(passing, passing, kv_recv.at[1, j]).wait()
            pltpu.make_async_remote_copy(
                src_ref=passing, dst_ref=kv_far.at[:, :, cols(j)], send_sem=pass_send, recv_sem=kv_recv.at[0, j],
                device_id=(inner, flipped, core), device_id_type=MESH,
            ).start()

        pltpu.make_async_copy(q_all.at[1, :, cols(j)], q_all.at[1, :, cols(j)], q_recv.at[j]).wait()
        pltpu.make_async_copy(kv_far.at[:, :, cols(j)], kv_far.at[:, :, cols(j)], kv_recv.at[0, j]).wait()
        g = core * heads + j
        block, logs = attend(q_all[1, :, cols(j)], j)
        o_out[j, :HD, :] = block
        o_out[j, HD:, :] = logs
        for c in range(2):
            pltpu.make_async_remote_copy(
                src_ref=o_out.at[j, :, halves(c)], dst_ref=part_far.at[g],
                send_sem=far_send, recv_sem=far_recv.at[g],
                device_id=(inner_up, outer, c), device_id_type=MESH,
            ).start()
        block, logs = attend(q_all[0, :, cols(j)], j)
        o_mine[j, :HD, :] = block
        o_mine[j, HD:, :] = logs
        pltpu.make_async_remote_copy(
            src_ref=o_mine.at[j, :, halves(other)], dst_ref=part_own.at[g],
            send_sem=mine_send, recv_sem=mine_recv.at[j],
            device_id=(inner, outer, other), device_id_type=MESH,
        ).start()
        part_own[g] = o_mine[j, :, halves(core)]

        @pl.when(j >= LAG)
        def _():
            merge(j - LAG)

        return 0

    lax.fori_loop(0, heads, head_step, 0)
    for j in range(heads - LAG, heads):
        merge(j)

    pltpu.make_async_copy(result, o_hbm, out_sem).wait()
    pltpu.make_async_copy(q_hbm, q_hbm, q_send).wait()
    pltpu.make_async_copy(k_hbm, k_hbm, kv_send.at[0]).wait()
    pltpu.make_async_copy(v_hbm, v_hbm, kv_send.at[1]).wait()
    pltpu.make_async_copy(o_out, o_out, far_send).wait()

    @pl.when(y == 0)
    def _():
        passed = kv_in.at[1, :, :, cols(0, (heads + 1) // 2)]
        pltpu.make_async_copy(passed, passed, pass_send).wait()

    pltpu.make_async_copy(o_mine.at[:, :, halves(0)], o_mine.at[:, :, halves(0)], mine_send).wait()


def solution(mesh):
    n_inner, n_outer = mesh.shape["inner"], mesh.shape["outer"]

    def per_device(q, k, v):
        rows, width = q.shape
        heads = width // HD // 2
        both = 2 * rows
        dma = pltpu.SemaphoreType.DMA
        return pl.pallas_call(
            functools.partial(kernel, n_inner, n_outer, heads),
            out_shape=jax.ShapeDtypeStruct((rows, width), jnp.bfloat16),
            in_specs=[pl.BlockSpec(memory_space=pltpu.HBM)] * 3,
            out_specs=pl.BlockSpec(memory_space=pl.ANY),
            scratch_shapes=[
                pltpu.VMEM((2, both, width // 2), jnp.bfloat16),
                pltpu.VMEM((2, both, width // 2), jnp.bfloat16),
                pltpu.VMEM((2, 2, both, width // 2), jnp.bfloat16),
                pltpu.VMEM((heads, HD + TAIL, both), jnp.bfloat16),
                pltpu.VMEM((heads, HD + TAIL, both), jnp.bfloat16),
                pltpu.VMEM((2 * heads, HD + TAIL, rows), jnp.bfloat16),
                pltpu.VMEM((2 * heads, HD + TAIL, rows), jnp.bfloat16),
                pltpu.VMEM((rows, width), jnp.bfloat16),
                dma((3,)), dma((3,)), dma((3,)),
                dma, dma((heads,)), dma((2,)), dma((2, heads)), dma,
                dma, dma((2 * heads,)), dma, dma((heads,)), dma,
            ],
            compiler_params=pltpu.CompilerParams(
                collective_id=0, has_side_effects=True, vmem_limit_bytes=56 << 20
            ),
        )(q, k, v)

    spec = P(("inner", "outer", "head"), None)
    return jax.shard_map(per_device, mesh=mesh, in_specs=(spec,) * 3, out_specs=spec, check_vma=False)
```

```python
import functools
import math

import jax
import jax.numpy as jnp
from jax import lax
from jax.experimental import pallas as pl
from jax.experimental.pallas import tpu as pltpu
from jax.sharding import PartitionSpec as P

HD = 128
MESH = pl.DeviceIdType.MESH
LANE = 128
TAIL = 16
LAG = 2
BACK, BACK_WRAP = 8, 6
ORDER_0 = (1, 0, 3, 2, 8, 9, 5, 4, 6, 7)
PASSES = (
    (("first", 8, (0, 1, 2, 3)), ("ring", 0, (0,)), ("first", 9, (0,))),
    (("first", 9, (1, 2, 3)),),
    (("first", 6, (2,)), ("second", 8, (0, 1, 3)), ("ring", 2, (0,)), ("second", 9, (0,))),
    (("first", 7, (2,)), ("second", 9, (1, 3))),
    (("second", 6, (1,)), ("second", 8, (2,))),
    (("second", 7, (1,)), ("second", 9, (2,)), ("ring", 4, (0,))),
)


def cols(at, count=1):
    return pl.ds(pl.multiple_of(at * HD, HD), count * HD)


def halves(at):
    return pl.ds(pl.multiple_of(at * LANE, LANE), LANE)


def split_sum(x):
    high = x.astype(jnp.bfloat16)
    rest = x - high.astype(jnp.float32)
    mid = rest.astype(jnp.bfloat16)
    low = (rest - mid.astype(jnp.float32)).astype(jnp.bfloat16)
    row = lax.broadcasted_iota(jnp.int32, (TAIL, x.shape[1]), 0)
    wide = [jnp.broadcast_to(part.astype(jnp.float32), (TAIL, x.shape[1])) for part in (high, mid, low)]
    tile = jnp.where(row == 0, wide[0], jnp.where(row == 1, wide[1], jnp.where(row == 2, wide[2], 0.0)))
    return tile.astype(jnp.bfloat16)


def kernel(
    n_inner, n_outer, heads,
    q_hbm, k_hbm, v_hbm, o_hbm,
    q_all, kv_own, kv_in, o_out, o_mine, part_own, part_far, result,
    own_sem, swap_send, swap_recv, q_send, q_recv, kv_send, kv_recv, pass_send,
    far_send, far_recv, mine_send, mine_recv, out_sem,
):
    inner, outer, core = lax.axis_index("inner"), lax.axis_index("outer"), lax.axis_index("head")
    rows = q_hbm.shape[0]
    other = 1 - core
    inner_up, inner_down = lax.rem(inner + 1, n_inner), lax.rem(inner + n_inner - 1, n_inner)
    outer_up, outer_down = lax.rem(outer + 1, n_outer), lax.rem(outer + n_outer - 1, n_outer)
    along = n_outer // 2
    side, y = outer // along, lax.rem(outer, along)
    flipped = (1 - side) * along + y
    y_up, y_down = lax.rem(y + 1, along), lax.rem(y + along - 1, along)
    ring_up, ring_down = side * along + y_up, side * along + y_down
    cross_up, cross_down = (1 - side) * along + y_up, (1 - side) * along + y_down
    kv_far = kv_in.at[0]
    my_rows = pl.ds(pl.multiple_of(core * rows, rows), rows)

    own = []
    for at, (src, dst) in enumerate(((q_hbm, q_all.at[0]), (k_hbm, kv_own.at[0]), (v_hbm, kv_own.at[1]))):
        copy = pltpu.make_async_copy(src.at[:, cols(core * heads, heads)], dst.at[my_rows, :], own_sem.at[at])
        copy.start()
        own.append(copy)

    barrier = pltpu.get_barrier_semaphore()
    greeted = [(inner, outer, other)]
    for c in range(2):
        greeted += [(inner_up, outer, c), (inner_down, outer, c), (inner, outer_up, c), (inner, outer_down, c)]
        greeted += [(inner, ring_up, c), (inner, ring_down, c)]
    greeted += [(inner, at, core) for at in (flipped, cross_up, cross_down)]
    for device in greeted:
        pl.semaphore_signal(barrier, inc=1, device_id=device, device_id_type=MESH)
    pl.semaphore_wait(barrier, len(greeted))

    swaps = []
    for at, (src, dst) in enumerate(((q_hbm, q_all.at[0]), (k_hbm, kv_own.at[0]), (v_hbm, kv_own.at[1]))):
        copy = pltpu.make_async_remote_copy(
            src_ref=src.at[:, cols(other * heads, heads)], dst_ref=dst.at[my_rows, :],
            send_sem=swap_send.at[at], recv_sem=swap_recv.at[at],
            device_id=(inner, outer, other), device_id_type=MESH,
        )
        copy.start()
        swaps.append(copy)

    def send_head(n, _):
        late = jnp.where(n == heads - 1, 5, BACK_WRAP + lax.rem(n // 2 + 2, heads - BACK_WRAP))
        last = y == along - 1
        j = jnp.where(last, jnp.where(lax.rem(n, 2) == 0, n // 2, late), lax.rem(n + BACK, heads))
        for c in range(2):
            pltpu.make_async_remote_copy(
                src_ref=q_hbm.at[:, cols(c * heads + j)], dst_ref=q_all.at[1, my_rows, cols(j)],
                send_sem=q_send, recv_sem=q_recv.at[j],
                device_id=(inner_down, outer, c), device_id_type=MESH,
            ).start()
        back = jnp.where(j >= BACK, 1, jnp.where(last & (j >= BACK_WRAP), 1, 0))
        by_ring = jnp.where(last & (back == 0) & (lax.rem(j, 2) == 0), 1, 0)
        target = jnp.where(back == 1, ring_down, jnp.where(by_ring == 1, ring_up, outer_up))
        place = back + by_ring
        for at, src in enumerate((k_hbm, v_hbm)):
            for c in range(2):
                pltpu.make_async_remote_copy(
                    src_ref=src.at[:, cols(c * heads + j)], dst_ref=kv_in.at[place, at, my_rows, cols(j)],
                    send_sem=kv_send.at[at], recv_sem=kv_recv.at[place, j],
                    device_id=(inner, target, c), device_id_type=MESH,
                ).start()
        return 0

    lax.fori_loop(0, heads, send_head, 0)

    for copy in own:
        copy.wait()
    for copy in swaps:
        copy.wait()

    factor = math.log2(math.e) / math.sqrt(HD)

    def attend(q, j):
        keys = (kv_own[0, :, cols(j)], kv_in[0, 0, :, cols(j)])
        values = (kv_own[1, :, cols(j)], kv_in[0, 1, :, cols(j)])
        scores = [
            lax.dot_general(k, q, (((1,), (1,)), ((), ())), preferred_element_type=jnp.float32) for k in keys
        ]
        top = jnp.max(jnp.maximum(scores[0], scores[1]), axis=0, keepdims=True)
        weights = [jnp.exp2((s - top) * factor) for s in scores]
        total = jnp.sum(weights[0] + weights[1], axis=0, keepdims=True)
        summed = sum(
            lax.dot_general(
                v, w.astype(jnp.bfloat16), (((0,), (0,)), ((), ())), preferred_element_type=jnp.float32
            )
            for v, w in zip(values, weights)
        )
        return (summed * (1.0 / total)).astype(jnp.bfloat16), split_sum(top * factor + jnp.log2(total))

    def merge(j):
        for c in range(2):
            g = c * heads + j
            pltpu.make_async_copy(part_far.at[g], part_far.at[g], far_recv.at[g]).wait()

        pltpu.make_async_copy(
            part_own.at[other * heads + j], part_own.at[other * heads + j], mine_recv.at[j]
        ).wait()
        for c in range(2):
            g = c * heads + j
            logs = []
            for part in (part_own, part_far):
                tile = part[g, HD:, :].astype(jnp.float32)
                logs.append(tile[0:1] + tile[1:2] + tile[2:3])
            share_own = 1.0 / (1.0 + jnp.exp2(logs[1] - logs[0]))
            share_far = 1.0 / (1.0 + jnp.exp2(logs[0] - logs[1]))
            mixed = (
                part_own[g, :HD, :].astype(jnp.float32) * share_own
                + part_far[g, :HD, :].astype(jnp.float32) * share_far
            )
            result[:, cols(g)] = mixed.T.astype(jnp.bfloat16)
            pltpu.make_async_copy(result.at[:, cols(g)], o_hbm.at[:, cols(g)], out_sem).start()

    def pass_on(kind, j):
        source, place, target = {
            "first": (1, 2, ring_down if j % 2 else jnp.where(y == 2, cross_down, ring_down)),
            "second": (2, 0, jnp.where(y == 1, cross_down, ring_down) if j % 2 else ring_down),
            "ring": (1, 0, flipped),
        }[kind]
        block = kv_in.at[source, :, :, cols(j)]
        pltpu.make_async_copy(block, block, kv_recv.at[source, j]).wait()
        pltpu.make_async_remote_copy(
            src_ref=block, dst_ref=kv_in.at[place, :, :, cols(j)], send_sem=pass_send, recv_sem=kv_recv.at[place, j],
            device_id=(inner, target, core), device_id_type=MESH,
        ).start()

    def head_at(n):
        first = ORDER_0[0]
        for at, j in enumerate(ORDER_0):
            first = jnp.where(n == at, j, first)
        return jnp.where(y == 0, first, n)

    def head_step(n, _):
        for at, passes in enumerate(PASSES):

            @pl.when(n == at)
            def _():
                for kind, which, ys in passes:

                    @pl.when(functools.reduce(jnp.logical_or, [y == own_y for own_y in ys]))
                    def _():
                        pass_on(kind, which)

        j = head_at(n)
        pltpu.make_async_copy(q_all.at[1, :, cols(j)], q_all.at[1, :, cols(j)], q_recv.at[j]).wait()
        pltpu.make_async_copy(kv_far.at[:, :, cols(j)], kv_far.at[:, :, cols(j)], kv_recv.at[0, j]).wait()
        g = core * heads + j
        block, logs = attend(q_all[1, :, cols(j)], j)
        o_out[j, :HD, :] = block
        o_out[j, HD:, :] = logs
        for c in range(2):
            pltpu.make_async_remote_copy(
                src_ref=o_out.at[j, :, halves(c)], dst_ref=part_far.at[g],
                send_sem=far_send, recv_sem=far_recv.at[g],
                device_id=(inner_up, outer, c), device_id_type=MESH,
            ).start()
        block, logs = attend(q_all[0, :, cols(j)], j)
        o_mine[j, :HD, :] = block
        o_mine[j, HD:, :] = logs
        pltpu.make_async_remote_copy(
            src_ref=o_mine.at[j, :, halves(other)], dst_ref=part_own.at[g],
            send_sem=mine_send, recv_sem=mine_recv.at[j],
            device_id=(inner, outer, other), device_id_type=MESH,
        ).start()
        part_own[g] = o_mine[j, :, halves(core)]

        @pl.when(n >= LAG)
        def _():
            merge(head_at(n - LAG))

        return 0

    lax.fori_loop(0, heads, head_step, 0)
    for n in range(heads - LAG, heads):
        merge(head_at(n))

    pltpu.make_async_copy(result, o_hbm, out_sem).wait()
    pltpu.make_async_copy(q_hbm, q_hbm, q_send).wait()
    pltpu.make_async_copy(k_hbm, k_hbm, kv_send.at[0]).wait()
    pltpu.make_async_copy(v_hbm, v_hbm, kv_send.at[1]).wait()
    pltpu.make_async_copy(o_out, o_out, far_send).wait()

    for own_y in range(along):
        count = sum(own_y in ys for passes in PASSES for _, _, ys in passes)

        @pl.when(y == own_y)
        def _():
            passed = kv_in.at[1, :, :, cols(0, count)]
            pltpu.make_async_copy(passed, passed, pass_send).wait()

    pltpu.make_async_copy(o_mine.at[:, :, halves(0)], o_mine.at[:, :, halves(0)], mine_send).wait()


def solution(mesh):
    n_inner, n_outer = mesh.shape["inner"], mesh.shape["outer"]

    def per_device(q, k, v):
        rows, width = q.shape
        heads = width // HD // 2
        both = 2 * rows
        dma = pltpu.SemaphoreType.DMA
        return pl.pallas_call(
            functools.partial(kernel, n_inner, n_outer, heads),
            out_shape=jax.ShapeDtypeStruct((rows, width), jnp.bfloat16),
            in_specs=[pl.BlockSpec(memory_space=pltpu.HBM)] * 3,
            out_specs=pl.BlockSpec(memory_space=pl.ANY),
            scratch_shapes=[
                pltpu.VMEM((2, both, width // 2), jnp.bfloat16),
                pltpu.VMEM((2, both, width // 2), jnp.bfloat16),
                pltpu.VMEM((3, 2, both, width // 2), jnp.bfloat16),
                pltpu.VMEM((heads, HD + TAIL, both), jnp.bfloat16),
                pltpu.VMEM((heads, HD + TAIL, both), jnp.bfloat16),
                pltpu.VMEM((2 * heads, HD + TAIL, rows), jnp.bfloat16),
                pltpu.VMEM((2 * heads, HD + TAIL, rows), jnp.bfloat16),
                pltpu.VMEM((rows, width), jnp.bfloat16),
                dma((3,)), dma((3,)), dma((3,)),
                dma, dma((heads,)), dma((2,)), dma((3, heads)), dma,
                dma, dma((2 * heads,)), dma, dma((heads,)), dma,
            ],
            compiler_params=pltpu.CompilerParams(
                collective_id=0, has_side_effects=True, vmem_limit_bytes=56 << 20
            ),
        )(q, k, v)

    spec = P(("inner", "outer", "head"), None)
    return jax.shard_map(per_device, mesh=mesh, in_specs=(spec,) * 3, out_specs=spec, check_vma=False)
```

```python
import functools
import math

import jax
import jax.numpy as jnp
from jax import lax
from jax.experimental import pallas as pl
from jax.experimental.pallas import tpu as pltpu
from jax.sharding import PartitionSpec as P

HD = 128
MESH = pl.DeviceIdType.MESH
LANE = 128
TAIL = 16
BACK, BACK_WRAP = 8, 5
EVERY = (0, 1, 2, 3)
PASSES = (
    (("first", 8, EVERY), ("first", 9, EVERY)), (("second", 8, (0, 2, 3)),), (("second", 9, (0, 2, 3)),), (("second", 9, (1,)),), (), (("second", 8, (1,)),),
)
PASSES_WRAP = (
    (("first", 8, EVERY), ("ring", 0, (0,)), ("first", 9, EVERY), ("ring", 1, (0,))),
    (("query", 0, EVERY), ("first", 6, (2,)), ("second", 8, (0, 1, 3)), ("ring", 2, (0,))),
    (("query", 1, EVERY), ("first", 7, (2,)), ("second", 9, (0, 1, 3)), ("ring", 3, (0,))),
    (("query", 2, EVERY), ("first", 5, (2,)), ("second", 6, (1,)), ("ring", 4, (0,))),
    (("second", 8, (2,)), ("second", 7, (1,))),
    (("second", 9, (2,)), ("second", 5, (1,))),
)
HOLD = 3
HANDED = (0, 4, 7, 10)
ORDER_WRAP = (0, 1, 2, 8, 3, 9, 6, 4, 7, 5)


def cols(at, count=1):
    return pl.ds(pl.multiple_of(at * HD, HD), count * HD)


def halves(at):
    return pl.ds(pl.multiple_of(at * LANE, LANE), LANE)


def split_sum(x):
    high = x.astype(jnp.bfloat16)
    rest = x - high.astype(jnp.float32)
    mid = rest.astype(jnp.bfloat16)
    low = (rest - mid.astype(jnp.float32)).astype(jnp.bfloat16)
    row = lax.broadcasted_iota(jnp.int32, (TAIL, x.shape[1]), 0)
    wide = [jnp.broadcast_to(part.astype(jnp.float32), (TAIL, x.shape[1])) for part in (high, mid, low)]
    tile = jnp.where(row == 0, wide[0], jnp.where(row == 1, wide[1], jnp.where(row == 2, wide[2], 0.0)))
    return tile.astype(jnp.bfloat16)


def kernel(
    n_inner, n_outer, heads,
    q_hbm, k_hbm, v_hbm, result,
    q_all, kv_own, kv_in, o_out, o_mine, part_own, part_far,
    entered, own_sem, swap_send, swap_recv, q_send, q_recv, hand_send, kv_send, kv_recv, pass_send,
    far_send, far_recv, mine_send, mine_recv,
):
    inner, outer, core = lax.axis_index("inner"), lax.axis_index("outer"), lax.axis_index("head")
    rows = q_hbm.shape[0]
    other = 1 - core
    inner_up, inner_down = lax.rem(inner + 1, n_inner), lax.rem(inner + n_inner - 1, n_inner)
    outer_up, outer_down = lax.rem(outer + 1, n_outer), lax.rem(outer + n_outer - 1, n_outer)
    along = n_outer // 2
    side, y = outer // along, lax.rem(outer, along)
    flipped = (1 - side) * along + y
    z = lax.rem(inner, n_inner // 2)
    far = n_inner // 2 - 1
    wrap = z == 0
    mate = lax.rem(inner + n_inner // 2, n_inner)
    below, above = lax.rem(inner + far, n_inner), lax.rem(inner + n_inner - far, n_inner)
    handing, handed = wrap & (y == along - 1), (z == far) & (y == along - 1)
    y_up, y_down = lax.rem(y + 1, along), lax.rem(y + along - 1, along)
    ring_up, ring_down = side * along + y_up, side * along + y_down
    cross_up, cross_down = (1 - side) * along + y_up, (1 - side) * along + y_down
    kv_far = kv_in.at[0]
    my_rows = pl.ds(pl.multiple_of(core * rows, rows), rows)

    own = []
    for at, (src, dst) in enumerate(((q_hbm, q_all.at[0]), (k_hbm, kv_own.at[0]), (v_hbm, kv_own.at[1]))):
        copy = pltpu.make_async_copy(src.at[:, cols(core * heads, heads)], dst.at[my_rows, :], own_sem.at[at])
        copy.start()
        own.append(copy)

    barrier = pltpu.get_barrier_semaphore()
    around = [(inner, outer, other)]
    for c in range(2):
        around += [(inner, at, c) for at in (outer_up, outer_down, ring_up, ring_down)]
    around += [(inner, at, core) for at in (flipped, cross_up, cross_down)]
    for device in around + [(inner_down, outer, c) for c in range(2)]:
        pl.semaphore_signal(barrier, inc=1, device_id=device, device_id_type=MESH)

    @pl.when(handing)
    def _():
        for at in (mate, below):
            for c in range(2):
                pl.semaphore_signal(barrier, inc=1, device_id=(at, outer, c), device_id_type=MESH)

    pl.semaphore_wait(barrier, len(around) + 2 + jnp.where(handing | handed, 2, 0))
    for c in range(2):
        device = (jnp.where(handed, above, inner_up), outer, c)
        pl.semaphore_signal(entered, inc=1, device_id=device, device_id_type=MESH)

    swaps = []
    for at, (src, dst) in enumerate(((q_hbm, q_all.at[0]), (k_hbm, kv_own.at[0]), (v_hbm, kv_own.at[1]))):
        copy = pltpu.make_async_remote_copy(
            src_ref=src.at[:, cols(other * heads, heads)], dst_ref=dst.at[my_rows, :],
            send_sem=swap_send.at[at], recv_sem=swap_recv.at[at],
            device_id=(inner, outer, other), device_id_type=MESH,
        )
        copy.start()
        swaps.append(copy)

    def send_head(n, _):
        late = jnp.where(n == heads - 1, BACK_WRAP, BACK_WRAP + 1 + lax.rem(n // 2 + 2, heads - BACK_WRAP - 1))
        last = (y == along - 1) & wrap
        j = jnp.where(last, jnp.where(lax.rem(n, 2) == 0, n // 2, late), lax.rem(n + BACK, heads))
        back = jnp.where(j >= BACK, 1, jnp.where(last & (j >= BACK_WRAP), 1, 0))
        by_ring = jnp.where(last & (back == 0), 1, 0)
        target = jnp.where(back == 1, ring_down, jnp.where(by_ring == 1, ring_up, outer_up))
        place = back + by_ring
        for at, src in enumerate((k_hbm, v_hbm)):
            for c in range(2):
                pltpu.make_async_remote_copy(
                    src_ref=src.at[:, cols(c * heads + j)], dst_ref=kv_in.at[place, at, my_rows, cols(j)],
                    send_sem=kv_send.at[at], recv_sem=kv_recv.at[place, j],
                    device_id=(inner, target, c), device_id_type=MESH,
                ).start()
        return 0

    q_place, q_target = jnp.where(handing, 2, 1), jnp.where(handing, mate, inner_down)

    def send_query(j, _):
        for c in range(2):
            pltpu.make_async_remote_copy(
                src_ref=q_hbm.at[:, cols(c * heads + j)], dst_ref=q_all.at[q_place, my_rows, cols(j)],
                send_sem=q_send, recv_sem=q_recv.at[q_place, j],
                device_id=(q_target, outer, c), device_id_type=MESH,
            ).start()
        return 0

    def hand_query(j, _):
        block = q_all.at[2, :, cols(j)]
        pltpu.make_async_copy(block, block, q_recv.at[2, j]).wait()
        pltpu.make_async_remote_copy(
            src_ref=block, dst_ref=q_all.at[1, :, cols(j)], send_sem=hand_send, recv_sem=q_recv.at[1, j],
            device_id=(below, outer, core), device_id_type=MESH,
        ).start()
        return 0

    @pl.when(handing)
    def _():
        lax.fori_loop(0, heads, send_query, 0)

    lax.fori_loop(0, heads, send_head, 0)

    @pl.when(z > 0)
    def _():
        pl.semaphore_wait(entered, 2)
        lax.fori_loop(0, heads, send_query, 0)

    for copy in own:
        copy.wait()
    for copy in swaps:
        copy.wait()

    factor = math.log2(math.e) / math.sqrt(HD)

    def attend(q, j):
        keys = (kv_own[0, :, cols(j)], kv_in[0, 0, :, cols(j)])
        values = (kv_own[1, :, cols(j)], kv_in[0, 1, :, cols(j)])
        scores = [
            lax.dot_general(k, q, (((1,), (1,)), ((), ())), preferred_element_type=jnp.float32) for k in keys
        ]
        top = jnp.max(jnp.maximum(scores[0], scores[1]), axis=0, keepdims=True)
        weights = [jnp.exp2((s - top) * factor) for s in scores]
        total = jnp.sum(weights[0] + weights[1], axis=0, keepdims=True)
        summed = sum(
            lax.dot_general(
                v, w.astype(jnp.bfloat16), (((0,), (0,)), ((), ())), preferred_element_type=jnp.float32
            )
            for v, w in zip(values, weights)
        )
        return (summed * (1.0 / total)).astype(jnp.bfloat16), split_sum(top * factor + jnp.log2(total))

    def merge(j):
        for c in range(2):
            g = c * heads + j
            pltpu.make_async_copy(part_far.at[g], part_far.at[g], far_recv.at[g]).wait()

        pltpu.make_async_copy(
            part_own.at[other * heads + j], part_own.at[other * heads + j], mine_recv.at[j]
        ).wait()
        for c in range(2):
            g = c * heads + j
            logs = []
            for part in (part_own, part_far):
                tile = part[g, HD:, :].astype(jnp.float32)
                logs.append(tile[0:1] + tile[1:2] + tile[2:3])
            share_own = 1.0 / (1.0 + jnp.exp2(logs[1] - logs[0]))
            share_far = 1.0 / (1.0 + jnp.exp2(logs[0] - logs[1]))
            mixed = (
                part_own[g, :HD, :].astype(jnp.float32) * share_own
                + part_far[g, :HD, :].astype(jnp.float32) * share_far
            )
            result[:, cols(g)] = mixed.T.astype(jnp.bfloat16)

    def pass_on(kind, j):
        source, place, target = {
            "first": (1, 2, jnp.where((y == 2) & wrap if j % 2 else y == 2, cross_down, ring_down)),
            "second": (2, 0, jnp.where((y == 1) & jnp.logical_not(wrap), cross_down, ring_down) if j % 2 else ring_down),
            "ring": (1, 0, flipped),
        }[kind]
        block = kv_in.at[source, :, :, cols(j)]
        pltpu.make_async_copy(block, block, kv_recv.at[source, j]).wait()
        pltpu.make_async_remote_copy(
            src_ref=block, dst_ref=kv_in.at[place, :, :, cols(j)], send_sem=pass_send, recv_sem=kv_recv.at[place, j],
            device_id=(inner, target, core), device_id_type=MESH,
        ).start()

    def head_at(n):
        order = ORDER_WRAP[0]
        for at, j in enumerate(ORDER_WRAP):
            order = jnp.where(n == at, j, order)
        return jnp.where((y == 0) & wrap, order, n)

    def run_passes(passes):
        for kind, which, ys in passes:

            @pl.when(functools.reduce(jnp.logical_or, [y == own_y for own_y in ys]))
            def _():
                if kind != "query":
                    pass_on(kind, which)
                    return

                if which == 0:
                    pl.semaphore_wait(entered, 2)

                    @pl.when(jnp.logical_not(handing))
                    def _():
                        lax.fori_loop(0, heads, send_query, 0)

                @pl.when(handing)
                def _():
                    lax.fori_loop(HANDED[which], HANDED[which + 1], hand_query, 0)

    def send_part(n, _):
        j = head_at(n)
        for c in range(2):
            pltpu.make_async_remote_copy(
                src_ref=o_out.at[j, :, halves(c)], dst_ref=part_far.at[core * heads + j],
                send_sem=far_send, recv_sem=far_recv.at[core * heads + j],
                device_id=(inner_up, outer, c), device_id_type=MESH,
            ).start()
        return 0

    def head_step(n, _):
        for table, here in ((PASSES, jnp.logical_not(wrap)), (PASSES_WRAP, wrap)):
            for at, passes in enumerate(table):

                @pl.when((n == at) & here)
                def _():
                    run_passes(passes)

        j = head_at(n)
        pltpu.make_async_copy(q_all.at[1, :, cols(j)], q_all.at[1, :, cols(j)], q_recv.at[1, j]).wait()
        pltpu.make_async_copy(kv_far.at[:, :, cols(j)], kv_far.at[:, :, cols(j)], kv_recv.at[0, j]).wait()
        g = core * heads + j
        block, logs = attend(q_all[1, :, cols(j)], j)
        o_out[j, :HD, :] = block
        o_out[j, HD:, :] = logs
        held = jnp.where(z == far, HOLD, 0)

        @pl.when(n >= held)
        def _():
            lax.fori_loop(jnp.where(n == held, 0, n), n + 1, send_part, 0)

        block, logs = attend(q_all[0, :, cols(j)], j)
        o_mine[j, :HD, :] = block
        o_mine[j, HD:, :] = logs
        pltpu.make_async_remote_copy(
            src_ref=o_mine.at[j, :, halves(other)], dst_ref=part_own.at[g],
            send_sem=mine_send, recv_sem=mine_recv.at[j],
            device_id=(inner, outer, other), device_id_type=MESH,
        ).start()
        part_own[g] = o_mine[j, :, halves(core)]

        return 0

    lax.fori_loop(0, heads, head_step, 0)
    lax.fori_loop(0, heads, lambda n, _: merge(n) or 0, 0)

    pltpu.make_async_copy(q_hbm, q_hbm, q_send).wait()

    @pl.when(handing)
    def _():
        pltpu.make_async_copy(q_all.at[2], q_all.at[2], hand_send).wait()

    pltpu.make_async_copy(k_hbm, k_hbm, kv_send.at[0]).wait()
    pltpu.make_async_copy(v_hbm, v_hbm, kv_send.at[1]).wait()
    pltpu.make_async_copy(o_out, o_out, far_send).wait()

    for own_y in range(along):
        for table, here in ((PASSES, jnp.logical_not(wrap)), (PASSES_WRAP, wrap)):
            count = sum(own_y in ys for passes in table for kind, _, ys in passes if kind != "query")

            @pl.when((y == own_y) & here)
            def _():
                passed = kv_in.at[1, :, :, cols(0, count)]
                pltpu.make_async_copy(passed, passed, pass_send).wait()

    pltpu.make_async_copy(o_mine.at[:, :, halves(0)], o_mine.at[:, :, halves(0)], mine_send).wait()


def solution(mesh):
    n_inner, n_outer = mesh.shape["inner"], mesh.shape["outer"]

    def per_device(q, k, v):
        rows, width = q.shape
        heads = width // HD // 2
        both = 2 * rows
        dma = pltpu.SemaphoreType.DMA
        return pl.pallas_call(
            functools.partial(kernel, n_inner, n_outer, heads),
            out_shape=jax.ShapeDtypeStruct((rows, width), jnp.bfloat16),
            in_specs=[pl.BlockSpec(memory_space=pltpu.HBM)] * 3,
            out_specs=pl.BlockSpec(memory_space=pltpu.VMEM),
            scratch_shapes=[
                pltpu.VMEM((3, both, width // 2), jnp.bfloat16),
                pltpu.VMEM((2, both, width // 2), jnp.bfloat16),
                pltpu.VMEM((3, 2, both, width // 2), jnp.bfloat16),
                pltpu.VMEM((heads, HD + TAIL, both), jnp.bfloat16),
                pltpu.VMEM((heads, HD + TAIL, both), jnp.bfloat16),
                pltpu.VMEM((2 * heads, HD + TAIL, rows), jnp.bfloat16),
                pltpu.VMEM((2 * heads, HD + TAIL, rows), jnp.bfloat16),
                pltpu.SemaphoreType.REGULAR, dma((3,)), dma((3,)), dma((3,)),
                dma, dma((3, heads)), dma, dma((2,)), dma((3, heads)), dma,
                dma, dma((2 * heads,)), dma, dma((heads,)),
            ],
            compiler_params=pltpu.CompilerParams(
                collective_id=0, has_side_effects=True, vmem_limit_bytes=53 << 20
            ),
        )(q, k, v)

    spec = P(("inner", "outer", "head"), None)
    return jax.shard_map(per_device, mesh=mesh, in_specs=(spec,) * 3, out_specs=spec, check_vma=False)
```

```python
import functools
import math

import jax
import jax.numpy as jnp
from jax import lax
from jax.experimental import pallas as pl
from jax.experimental.pallas import tpu as pltpu
from jax.sharding import PartitionSpec as P

HD = 128
MESH = pl.DeviceIdType.MESH
LANE = 128
STATS = 16
EARLY = 8
BACK, BACK_WRAP = 8, 5
EVERY = (0, 1, 2, 3)
PASSES = (
    (("first", 8, EVERY),), (("first", 9, EVERY), ("second", 8, EVERY),), (("second", 9, EVERY),),
)
PASSES_FAR = (
    (("first", 8, EVERY), ("first", 9, EVERY), ("second", 8, (1, 2, 3)), ("second", 9, (1, 2, 3))),
    (("second", 8, (0,)),), (("second", 9, (0,)),),
)
PASSES_WRAP = (
    (("first", 8, EVERY), ("ring", 0, (0,)), ("first", 9, EVERY), ("query", 0, EVERY), ("ring", 1, (0,))),
    (("query", 1, EVERY), ("first", 6, (2,)), ("second", 8, (0, 1, 3)), ("ring", 2, (0,))),
    (("query", 2, EVERY), ("first", 7, (2,)), ("second", 9, (0, 1, 3)), ("ring", 3, (0,))),
    (("first", 5, (2,)), ("second", 6, (1,)), ("ring", 4, (0,))),
    (("second", 8, (2,)), ("second", 7, (1,))),
    (("second", 9, (2,)), ("second", 5, (1,))),
)
HOLD = (0, 0, 1, 0)
HANDED = (0, 3, 6, 10)
ORDER = (0, 1, 2, 3, 4, 8, 5, 9, 6, 7)
ORDER_WRAP = (0, 1, 2, 8, 3, 9, 6, 4, 7, 5)


def cols(at, count=1):
    return pl.ds(pl.multiple_of(at * HD, HD), count * HD)


def halves(at):
    return pl.ds(pl.multiple_of(at * LANE, LANE), LANE)


def kernel(
    n_inner, n_outer, heads,
    q_hbm, k_hbm, v_hbm, result,
    q_all, kv_own, kv_in, o_out, o_mine, part_own, part_far, sums_out, sums_mine, sums_own, sums_far,
    entered, own_sem, swap_send, swap_recv, q_send, q_recv, hand_send, kv_send, kv_recv, pass_send,
    far_send, far_recv, mine_send, mine_recv, sums_send, sums_recv, table_sem,
):
    inner, outer, core = lax.axis_index("inner"), lax.axis_index("outer"), lax.axis_index("head")
    rows = q_hbm.shape[0]
    other = 1 - core
    inner_up, inner_down = lax.rem(inner + 1, n_inner), lax.rem(inner + n_inner - 1, n_inner)
    outer_up, outer_down = lax.rem(outer + 1, n_outer), lax.rem(outer + n_outer - 1, n_outer)
    along = n_outer // 2
    side, y = outer // along, lax.rem(outer, along)
    flipped = (1 - side) * along + y
    z = lax.rem(inner, n_inner // 2)
    far = n_inner // 2 - 1
    wrap = z == 0
    mate = lax.rem(inner + n_inner // 2, n_inner)
    below, above = lax.rem(inner + far, n_inner), lax.rem(inner + n_inner - far, n_inner)
    by_mate = (y == along - 1) | (y == 1)
    handing, handed = wrap & by_mate, (z == far) & by_mate
    y_up, y_down = lax.rem(y + 1, along), lax.rem(y + along - 1, along)
    ring_up, ring_down = side * along + y_up, side * along + y_down
    cross_up, cross_down = (1 - side) * along + y_up, (1 - side) * along + y_down
    kv_far = kv_in.at[0]
    my_rows = pl.ds(pl.multiple_of(core * rows, rows), rows)

    own = []
    for at, (src, dst) in enumerate(((q_hbm, q_all.at[0]), (k_hbm, kv_own.at[0]), (v_hbm, kv_own.at[1]))):
        copy = pltpu.make_async_copy(src.at[:, cols(core * heads, heads)], dst.at[my_rows, :], own_sem.at[at])
        copy.start()
        own.append(copy)

    barrier = pltpu.get_barrier_semaphore()
    around = [(inner, outer, other)]
    for c in range(2):
        around += [(inner, at, c) for at in (outer_up, outer_down, ring_up, ring_down)]
    around += [(inner, at, core) for at in (flipped, cross_up, cross_down)]
    for device in around + [(inner_down, outer, c) for c in range(2)]:
        pl.semaphore_signal(barrier, inc=1, device_id=device, device_id_type=MESH)

    @pl.when(handing)
    def _():
        for at in (mate, below):
            for c in range(2):
                pl.semaphore_signal(barrier, inc=1, device_id=(at, outer, c), device_id_type=MESH)

    pl.semaphore_wait(barrier, len(around) + 2 + jnp.where(handing | handed, 2, 0))
    for c in range(2):
        device = (jnp.where(handed, above, inner_up), outer, c)
        pl.semaphore_signal(entered, inc=1, device_id=device, device_id_type=MESH)

    swaps = []
    for at, (src, dst) in enumerate(((q_hbm, q_all.at[0]), (k_hbm, kv_own.at[0]), (v_hbm, kv_own.at[1]))):
        copy = pltpu.make_async_remote_copy(
            src_ref=src.at[:, cols(other * heads, heads)], dst_ref=dst.at[my_rows, :],
            send_sem=swap_send.at[at], recv_sem=swap_recv.at[at],
            device_id=(inner, outer, other), device_id_type=MESH,
        )
        copy.start()
        swaps.append(copy)

    def send_head(n, _):
        late = jnp.where(n == heads - 1, BACK_WRAP, BACK_WRAP + 1 + lax.rem(n // 2 + 2, heads - BACK_WRAP - 1))
        last = (y == along - 1) & wrap
        j = jnp.where(last, jnp.where(lax.rem(n, 2) == 0, n // 2, late), lax.rem(n + BACK, heads))
        back = jnp.where(j >= BACK, 1, jnp.where(last & (j >= BACK_WRAP), 1, 0))
        by_ring = jnp.where(last & (back == 0), 1, 0)
        target = jnp.where(back == 1, ring_down, jnp.where(by_ring == 1, ring_up, outer_up))
        place = back + by_ring
        for at, src in enumerate((k_hbm, v_hbm)):
            for c in range(2):
                pltpu.make_async_remote_copy(
                    src_ref=src.at[:, cols(c * heads + j)], dst_ref=kv_in.at[place, at, my_rows, cols(j)],
                    send_sem=kv_send.at[at], recv_sem=kv_recv.at[place, j],
                    device_id=(inner, target, c), device_id_type=MESH,
                ).start()
        return 0

    q_place, q_target = jnp.where(handing, 2, 1), jnp.where(handing, mate, inner_down)

    def send_query(j, _):
        for c in range(2):
            pltpu.make_async_remote_copy(
                src_ref=q_hbm.at[:, cols(c * heads + j)], dst_ref=q_all.at[q_place, my_rows, cols(j)],
                send_sem=q_send, recv_sem=q_recv.at[q_place, j],
                device_id=(q_target, outer, c), device_id_type=MESH,
            ).start()
        return 0

    def hand_query(j, _):
        block = q_all.at[2, :, cols(j)]
        pltpu.make_async_copy(block, block, q_recv.at[2, j]).wait()
        pltpu.make_async_remote_copy(
            src_ref=block, dst_ref=q_all.at[1, :, cols(j)], send_sem=hand_send, recv_sem=q_recv.at[1, j],
            device_id=(below, outer, core), device_id_type=MESH,
        ).start()
        return 0

    @pl.when(handing)
    def _():
        lax.fori_loop(0, heads, send_query, 0)

    lax.fori_loop(0, heads, send_head, 0)

    @pl.when(z > 0)
    def _():
        pl.semaphore_wait(entered, 2)
        lax.fori_loop(0, heads, send_query, 0)

    for copy in own:
        copy.wait()
    for copy in swaps:
        copy.wait()

    factor = math.log2(math.e) / math.sqrt(HD)

    def attend(q, j):
        keys = (kv_own[0, :, cols(j)], kv_in[0, 0, :, cols(j)])
        values = (kv_own[1, :, cols(j)], kv_in[0, 1, :, cols(j)])
        scores = [
            lax.dot_general(k, q, (((1,), (1,)), ((), ())), preferred_element_type=jnp.float32) for k in keys
        ]
        top = jnp.max(jnp.maximum(scores[0], scores[1]), axis=0, keepdims=True)
        weights = [jnp.exp2((s - top) * factor) for s in scores]
        total = jnp.sum(weights[0] + weights[1], axis=0, keepdims=True)
        summed = sum(
            lax.dot_general(
                v, w.astype(jnp.bfloat16), (((0,), (0,)), ((), ())), preferred_element_type=jnp.float32
            )
            for v, w in zip(values, weights)
        )
        return (summed * (1.0 / total)).astype(jnp.bfloat16), top * factor + jnp.log2(total)

    def merge(n):
        j = sent_at(n)
        for c in range(2):
            g = c * heads + j
            pltpu.make_async_copy(part_far.at[g], part_far.at[g], far_recv.at[g]).wait()

        pltpu.make_async_copy(
            part_own.at[other * heads + j], part_own.at[other * heads + j], mine_recv.at[j]
        ).wait()
        table = jnp.where(n < EARLY, 0, 1)
        for c in range(2):
            g = c * heads + j
            log_own, log_far = sums_own[c, pl.ds(j, 1), :], sums_far[table, c, pl.ds(j, 1), :]
            share_own = 1.0 / (1.0 + jnp.exp2(log_far - log_own))
            share_far = 1.0 / (1.0 + jnp.exp2(log_own - log_far))
            mixed = part_own[g].astype(jnp.float32) * share_own + part_far[g].astype(jnp.float32) * share_far
            result[:, cols(g)] = mixed.T.astype(jnp.bfloat16)

    def pass_on(kind, j):
        source, place, target = {
            "first": (1, 2, jnp.where((y == 2) & (wrap if j % 2 else z < far), cross_down, ring_down)),
            "second": (2, 0, jnp.where((y == 1) & (z > 0 if j % 2 else z == far), cross_down, ring_down)),
            "ring": (1, 0, flipped),
        }[kind]
        block = kv_in.at[source, :, :, cols(j)]
        pltpu.make_async_copy(block, block, kv_recv.at[source, j]).wait()
        pltpu.make_async_remote_copy(
            src_ref=block, dst_ref=kv_in.at[place, :, :, cols(j)], send_sem=pass_send, recv_sem=kv_recv.at[place, j],
            device_id=(inner, target, core), device_id_type=MESH,
        ).start()

    def listed(order, n):
        head = order[0]
        for at, j in enumerate(order):
            head = jnp.where(n == at, j, head)
        return head

    def pick(by_y):
        return listed(by_y, y)

    def head_at(n):
        return jnp.where(wrap, jnp.where(y == 0, listed(ORDER_WRAP, n), n), listed(ORDER, n))

    def sent_at(n):
        return jnp.where(z == 1, jnp.where(y == 0, listed(ORDER_WRAP, n), n), listed(ORDER, n))

    def send_sums(table):
        for c in range(2):
            pltpu.make_async_remote_copy(
                src_ref=sums_out.at[table, :, halves(c)], dst_ref=sums_far.at[table, core],
                send_sem=sums_send.at[table], recv_sem=sums_recv.at[table, core],
                device_id=(inner_up, outer, c), device_id_type=MESH,
            ).start()

    def run_passes(passes):
        for kind, which, ys in passes:

            @pl.when(functools.reduce(jnp.logical_or, [y == own_y for own_y in ys]))
            def _():
                if kind != "query":
                    pass_on(kind, which)
                    return

                if which == 0:
                    pl.semaphore_wait(entered, 2)

                @pl.when(jnp.logical_not(handing))
                def _():
                    lax.fori_loop(HANDED[which], HANDED[which + 1], send_query, 0)

                @pl.when(handing)
                def _():
                    lax.fori_loop(HANDED[which], HANDED[which + 1], hand_query, 0)

    def send_part(n, _):
        j = head_at(n)
        for c in range(2):
            pltpu.make_async_remote_copy(
                src_ref=o_out.at[j, :, halves(c)], dst_ref=part_far.at[core * heads + j],
                send_sem=far_send, recv_sem=far_recv.at[core * heads + j],
                device_id=(inner_up, outer, c), device_id_type=MESH,
            ).start()
        return 0

    def head_step(n, _):
        for table, here in ((PASSES, (z > 0) & (z < far)), (PASSES_FAR, z == far), (PASSES_WRAP, wrap)):
            for at, passes in enumerate(table):

                @pl.when((n == at) & here)
                def _():
                    run_passes(passes)

        j = head_at(n)
        pltpu.make_async_copy(q_all.at[1, :, cols(j)], q_all.at[1, :, cols(j)], q_recv.at[1, j]).wait()
        pltpu.make_async_copy(kv_far.at[:, :, cols(j)], kv_far.at[:, :, cols(j)], kv_recv.at[0, j]).wait()
        g = core * heads + j
        block, logs = attend(q_all[1, :, cols(j)], j)
        o_out[j] = block

        @pl.when(n < EARLY)
        def _():
            sums_out[0, pl.ds(j, 1), :] = logs

        sums_out[1, pl.ds(j, 1), :] = logs

        @pl.when(n == EARLY - 1)
        def _():
            send_sums(0)

        @pl.when(n == heads - 1)
        def _():
            send_sums(1)

        held = jnp.where(z == far, pick(HOLD), 0)

        @pl.when(n >= held)
        def _():
            lax.fori_loop(jnp.where(n == held, 0, n), n + 1, send_part, 0)

        block, logs = attend(q_all[0, :, cols(j)], j)
        o_mine[j] = block
        sums_mine[pl.ds(j, 1), :] = logs
        pltpu.make_async_remote_copy(
            src_ref=o_mine.at[j, :, halves(other)], dst_ref=part_own.at[g],
            send_sem=mine_send, recv_sem=mine_recv.at[j],
            device_id=(inner, outer, other), device_id_type=MESH,
        ).start()
        part_own[g] = o_mine[j, :, halves(core)]

        return 0

    lax.fori_loop(0, heads, head_step, 0)
    sums_own[core] = sums_mine[:, halves(core)]
    swap = pltpu.make_async_remote_copy(
        src_ref=sums_mine.at[:, halves(other)], dst_ref=sums_own.at[core],
        send_sem=table_sem.at[0], recv_sem=table_sem.at[1],
        device_id=(inner, outer, other), device_id_type=MESH,
    )
    swap.start()
    swap.wait()

    def wait_sums(table):
        for c in range(2):
            pltpu.make_async_copy(sums_far.at[table, c], sums_far.at[table, c], sums_recv.at[table, c]).wait()

    wait_sums(0)
    lax.fori_loop(0, EARLY, lambda n, _: merge(n) or 0, 0)
    wait_sums(1)
    lax.fori_loop(EARLY, heads, lambda n, _: merge(n) or 0, 0)

    pltpu.make_async_copy(q_hbm, q_hbm, q_send).wait()

    @pl.when(handing)
    def _():
        pltpu.make_async_copy(q_all.at[2], q_all.at[2], hand_send).wait()

    pltpu.make_async_copy(k_hbm, k_hbm, kv_send.at[0]).wait()
    pltpu.make_async_copy(v_hbm, v_hbm, kv_send.at[1]).wait()
    pltpu.make_async_copy(o_out, o_out, far_send).wait()
    for table in range(2):
        pltpu.make_async_copy(sums_out.at[table], sums_out.at[table], sums_send.at[table]).wait()


    for own_y in range(along):
        for table, here in ((PASSES, (z > 0) & (z < far)), (PASSES_FAR, z == far), (PASSES_WRAP, wrap)):
            count = sum(own_y in ys for passes in table for kind, _, ys in passes if kind != "query")

            @pl.when((y == own_y) & here)
            def _():
                passed = kv_in.at[1, :, :, cols(0, count)]
                pltpu.make_async_copy(passed, passed, pass_send).wait()

    pltpu.make_async_copy(o_mine.at[:, :, halves(0)], o_mine.at[:, :, halves(0)], mine_send).wait()


def solution(mesh):
    n_inner, n_outer = mesh.shape["inner"], mesh.shape["outer"]

    def per_device(q, k, v):
        rows, width = q.shape
        heads = width // HD // 2
        both = 2 * rows
        dma = pltpu.SemaphoreType.DMA
        return pl.pallas_call(
            functools.partial(kernel, n_inner, n_outer, heads),
            out_shape=jax.ShapeDtypeStruct((rows, width), jnp.bfloat16),
            in_specs=[pl.BlockSpec(memory_space=pltpu.HBM)] * 3,
            out_specs=pl.BlockSpec(memory_space=pltpu.VMEM),
            scratch_shapes=[
                pltpu.VMEM((3, both, width // 2), jnp.bfloat16),
                pltpu.VMEM((2, both, width // 2), jnp.bfloat16),
                pltpu.VMEM((3, 2, both, width // 2), jnp.bfloat16),
                pltpu.VMEM((heads, HD, both), jnp.bfloat16),
                pltpu.VMEM((heads, HD, both), jnp.bfloat16),
                pltpu.VMEM((2 * heads, HD, rows), jnp.bfloat16),
                pltpu.VMEM((2 * heads, HD, rows), jnp.bfloat16),
                pltpu.VMEM((2, STATS, both), jnp.float32),
                pltpu.VMEM((STATS, both), jnp.float32),
                pltpu.VMEM((2, STATS, rows), jnp.float32),
                pltpu.VMEM((2, 2, STATS, rows), jnp.float32),
                pltpu.SemaphoreType.REGULAR, dma((3,)), dma((3,)), dma((3,)),
                dma, dma((3, heads)), dma, dma((2,)), dma((3, heads)), dma,
                dma, dma((2 * heads,)), dma, dma((heads,)), dma((2,)), dma((2, 2)), dma((2,)),
            ],
            compiler_params=pltpu.CompilerParams(
                collective_id=0, has_side_effects=True, vmem_limit_bytes=53 << 20
            ),
        )(q, k, v)

    spec = P(("inner", "outer", "head"), None)
    return jax.shard_map(per_device, mesh=mesh, in_specs=(spec,) * 3, out_specs=spec, check_vma=False)
```

```python
import functools
import math

import jax
import jax.numpy as jnp
from jax import lax
from jax.experimental import pallas as pl
from jax.experimental.pallas import tpu as pltpu
from jax.sharding import PartitionSpec as P

HD = 128
MESH = pl.DeviceIdType.MESH
LANE = 128
STATS = 16
EARLY = 8
BACK, BACK_WRAP = 8, 5
EVERY = (0, 1, 2, 3)
PASSES = (
    (("first", 8, EVERY),), (("first", 9, EVERY), ("second", 8, EVERY),), (("second", 9, EVERY),),
)
PASSES_FAR = (
    (("first", 8, EVERY), ("first", 9, EVERY), ("second", 8, (1, 2, 3)), ("second", 9, (1, 2, 3))),
    (("second", 8, (0,)),), (("second", 9, (0,)),),
)
PASSES_WRAP = (
    (("first", 8, EVERY), ("ring", 0, (0,)), ("first", 9, EVERY), ("query", 0, EVERY), ("ring", 1, (0,))),
    (("query", 1, EVERY), ("first", 6, (2,)), ("second", 8, (0, 1, 3)), ("ring", 2, (0,))),
    (("query", 2, EVERY), ("first", 7, (2,)), ("second", 9, (0, 1, 3)), ("ring", 3, (0,))),
    (("first", 5, (2,)), ("second", 6, (1,)), ("ring", 4, (0,))),
    (("second", 8, (2,)), ("second", 7, (1,))),
    (("second", 9, (2,)), ("second", 5, (1,))),
)
HOLD = (0, 0, 1, 0)
HANDED = (0, 3, 6, 10)
ORDER = (0, 1, 2, 3, 4, 8, 5, 9, 6, 7)
ORDER_WRAP = (0, 1, 2, 8, 3, 9, 6, 4, 7, 5)


def cols(at, count=1):
    return pl.ds(pl.multiple_of(at * HD, HD), count * HD)


def halves(at):
    return pl.ds(pl.multiple_of(at * LANE, LANE), LANE)


def kernel(
    n_inner, n_outer, heads,
    q_hbm, k_hbm, v_hbm, result,
    q_all, kv_own, kv_in, o_out, o_mine, part_own, part_far, sums_out, sums_mine, sums_own, sums_far,
    entered, own_sem, swap_send, swap_recv, q_send, q_recv, hand_send, kv_send, kv_recv, pass_send,
    far_send, far_recv, mine_send, mine_recv, sums_send, sums_recv, table_sem,
):
    inner, outer, core = lax.axis_index("inner"), lax.axis_index("outer"), lax.axis_index("head")
    rows = q_hbm.shape[0]
    other = 1 - core
    inner_up, inner_down = lax.rem(inner + 1, n_inner), lax.rem(inner + n_inner - 1, n_inner)
    outer_up, outer_down = lax.rem(outer + 1, n_outer), lax.rem(outer + n_outer - 1, n_outer)
    along = n_outer // 2
    side, y = outer // along, lax.rem(outer, along)
    flipped = (1 - side) * along + y
    z = lax.rem(inner, n_inner // 2)
    far = n_inner // 2 - 1
    wrap = z == 0
    mate = lax.rem(inner + n_inner // 2, n_inner)
    below, above = lax.rem(inner + far, n_inner), lax.rem(inner + n_inner - far, n_inner)
    by_mate = (y == along - 1) | (y == 1)
    handing, handed = wrap & by_mate, (z == far) & by_mate
    y_up, y_down = lax.rem(y + 1, along), lax.rem(y + along - 1, along)
    ring_up, ring_down = side * along + y_up, side * along + y_down
    cross_up, cross_down = (1 - side) * along + y_up, (1 - side) * along + y_down
    kv_far = kv_in.at[0]
    my_rows = pl.ds(pl.multiple_of(core * rows, rows), rows)

    own = []
    for at, (src, dst) in enumerate(((q_hbm, q_all.at[0]), (k_hbm, kv_own.at[0]), (v_hbm, kv_own.at[1]))):
        copy = pltpu.make_async_copy(src.at[:, cols(core * heads, heads)], dst.at[my_rows, :], own_sem.at[at])
        copy.start()
        own.append(copy)

    barrier = pltpu.get_barrier_semaphore()
    around = [(inner, outer, other)]
    for c in range(2):
        around += [(inner, at, c) for at in (outer_up, outer_down, ring_up, ring_down)]
    around += [(inner, at, core) for at in (flipped, cross_up, cross_down)]
    for device in around + [(inner_down, outer, c) for c in range(2)]:
        pl.semaphore_signal(barrier, inc=1, device_id=device, device_id_type=MESH)

    @pl.when(handing)
    def _():
        for at in (mate, below):
            for c in range(2):
                pl.semaphore_signal(barrier, inc=1, device_id=(at, outer, c), device_id_type=MESH)

    pl.semaphore_wait(barrier, len(around) + 2 + jnp.where(handing | handed, 2, 0))
    for c in range(2):
        device = (jnp.where(handed, above, inner_up), outer, c)
        pl.semaphore_signal(entered, inc=1, device_id=device, device_id_type=MESH)

    swaps = []
    for at, (src, dst) in enumerate(((q_hbm, q_all.at[0]), (k_hbm, kv_own.at[0]), (v_hbm, kv_own.at[1]))):
        copy = pltpu.make_async_remote_copy(
            src_ref=src.at[:, cols(other * heads, heads)], dst_ref=dst.at[my_rows, :],
            send_sem=swap_send.at[at], recv_sem=swap_recv.at[at],
            device_id=(inner, outer, other), device_id_type=MESH,
        )
        copy.start()
        swaps.append(copy)

    def send_head(n, _):
        late = jnp.where(n == heads - 1, BACK_WRAP, BACK_WRAP + 1 + lax.rem(n // 2 + 2, heads - BACK_WRAP - 1))
        last = (y == along - 1) & wrap
        j = jnp.where(last, jnp.where(lax.rem(n, 2) == 0, n // 2, late), jnp.where(n == 0, 0, jnp.where(n <= heads - BACK, n + BACK - 1, n + BACK - heads)))
        back = jnp.where(j >= BACK, 1, jnp.where(last & (j >= BACK_WRAP), 1, 0))
        by_ring = jnp.where(last & (back == 0), 1, 0)
        target = jnp.where(back == 1, ring_down, jnp.where(by_ring == 1, ring_up, outer_up))
        place = back + by_ring
        for at, src in enumerate((k_hbm, v_hbm)):
            for c in range(2):
                pltpu.make_async_remote_copy(
                    src_ref=src.at[:, cols(c * heads + j)], dst_ref=kv_in.at[place, at, my_rows, cols(j)],
                    send_sem=kv_send.at[at], recv_sem=kv_recv.at[place, j],
                    device_id=(inner, target, c), device_id_type=MESH,
                ).start()
        return 0

    q_place, q_target = jnp.where(handing, 2, 1), jnp.where(handing, mate, inner_down)

    def send_query(j, _):
        for c in range(2):
            pltpu.make_async_remote_copy(
                src_ref=q_hbm.at[:, cols(c * heads + j)], dst_ref=q_all.at[q_place, my_rows, cols(j)],
                send_sem=q_send, recv_sem=q_recv.at[q_place, j],
                device_id=(q_target, outer, c), device_id_type=MESH,
            ).start()
        return 0

    def hand_query(j, _):
        block = q_all.at[2, :, cols(j)]
        pltpu.make_async_copy(block, block, q_recv.at[2, j]).wait()
        pltpu.make_async_remote_copy(
            src_ref=block, dst_ref=q_all.at[1, :, cols(j)], send_sem=hand_send, recv_sem=q_recv.at[1, j],
            device_id=(below, outer, core), device_id_type=MESH,
        ).start()
        return 0

    @pl.when(handing)
    def _():
        lax.fori_loop(0, heads, send_query, 0)

    lax.fori_loop(0, heads, send_head, 0)

    @pl.when(z > 0)
    def _():
        pl.semaphore_wait(entered, 2)
        lax.fori_loop(0, heads, send_query, 0)

    for copy in own:
        copy.wait()
    for copy in swaps:
        copy.wait()

    factor = math.log2(math.e) / math.sqrt(HD)

    def attend(q, j):
        keys = (kv_own[0, :, cols(j)], kv_in[0, 0, :, cols(j)])
        values = (kv_own[1, :, cols(j)], kv_in[0, 1, :, cols(j)])
        scores = [
            lax.dot_general(k, q, (((1,), (1,)), ((), ())), preferred_element_type=jnp.float32) for k in keys
        ]
        top = jnp.max(jnp.maximum(scores[0], scores[1]), axis=0, keepdims=True)
        weights = [jnp.exp2((s - top) * factor) for s in scores]
        total = jnp.sum(weights[0] + weights[1], axis=0, keepdims=True)
        summed = sum(
            lax.dot_general(
                v, w.astype(jnp.bfloat16), (((0,), (0,)), ((), ())), preferred_element_type=jnp.float32
            )
            for v, w in zip(values, weights)
        )
        return (summed * (1.0 / total)).astype(jnp.bfloat16), top * factor + jnp.log2(total)

    def merge(n):
        j = sent_at(n)
        for c in range(2):
            g = c * heads + j
            pltpu.make_async_copy(part_far.at[g], part_far.at[g], far_recv.at[g]).wait()

        pltpu.make_async_copy(
            part_own.at[other * heads + j], part_own.at[other * heads + j], mine_recv.at[j]
        ).wait()
        table = jnp.where(n < EARLY, 0, 1)
        for c in range(2):
            g = c * heads + j
            log_own, log_far = sums_own[c, pl.ds(j, 1), :], sums_far[table, c, pl.ds(j, 1), :]
            share_own = 1.0 / (1.0 + jnp.exp2(log_far - log_own))
            share_far = 1.0 / (1.0 + jnp.exp2(log_own - log_far))
            mixed = part_own[g].astype(jnp.float32) * share_own + part_far[g].astype(jnp.float32) * share_far
            result[:, cols(g)] = mixed.T.astype(jnp.bfloat16)

    def pass_on(kind, j):
        source, place, target = {
            "first": (1, 2, jnp.where((y == 2) & (wrap if j % 2 else z < far), cross_down, ring_down)),
            "second": (2, 0, jnp.where((y == 1) & (z > 0 if j % 2 else z == far), cross_down, ring_down)),
            "ring": (1, 0, flipped),
        }[kind]
        block = kv_in.at[source, :, :, cols(j)]
        pltpu.make_async_copy(block, block, kv_recv.at[source, j]).wait()
        pltpu.make_async_remote_copy(
            src_ref=block, dst_ref=kv_in.at[place, :, :, cols(j)], send_sem=pass_send, recv_sem=kv_recv.at[place, j],
            device_id=(inner, target, core), device_id_type=MESH,
        ).start()

    def listed(order, n):
        head = order[0]
        for at, j in enumerate(order):
            head = jnp.where(n == at, j, head)
        return head

    def pick(by_y):
        return listed(by_y, y)

    def head_at(n):
        return jnp.where(wrap, jnp.where(y == 0, listed(ORDER_WRAP, n), n), listed(ORDER, n))

    def sent_at(n):
        return jnp.where(z == 1, jnp.where(y == 0, listed(ORDER_WRAP, n), n), listed(ORDER, n))

    def send_sums(table):
        for c in range(2):
            pltpu.make_async_remote_copy(
                src_ref=sums_out.at[table, :, halves(c)], dst_ref=sums_far.at[table, core],
                send_sem=sums_send.at[table], recv_sem=sums_recv.at[table, core],
                device_id=(inner_up, outer, c), device_id_type=MESH,
            ).start()

    def run_passes(passes):
        for kind, which, ys in passes:

            @pl.when(functools.reduce(jnp.logical_or, [y == own_y for own_y in ys]))
            def _():
                if kind != "query":
                    pass_on(kind, which)
                    return

                if which == 0:
                    pl.semaphore_wait(entered, 2)

                @pl.when(jnp.logical_not(handing))
                def _():
                    lax.fori_loop(HANDED[which], HANDED[which + 1], send_query, 0)

                @pl.when(handing)
                def _():
                    lax.fori_loop(HANDED[which], HANDED[which + 1], hand_query, 0)

    def send_part(n, _):
        j = head_at(n)
        for c in range(2):
            pltpu.make_async_remote_copy(
                src_ref=o_out.at[j, :, halves(c)], dst_ref=part_far.at[core * heads + j],
                send_sem=far_send, recv_sem=far_recv.at[core * heads + j],
                device_id=(inner_up, outer, c), device_id_type=MESH,
            ).start()
        return 0

    def head_step(n, _):
        for table, here in ((PASSES, (z > 0) & (z < far)), (PASSES_FAR, z == far), (PASSES_WRAP, wrap)):
            for at, passes in enumerate(table):

                @pl.when((n == at) & here)
                def _():
                    run_passes(passes)

        j = head_at(n)
        pltpu.make_async_copy(q_all.at[1, :, cols(j)], q_all.at[1, :, cols(j)], q_recv.at[1, j]).wait()
        pltpu.make_async_copy(kv_far.at[:, :, cols(j)], kv_far.at[:, :, cols(j)], kv_recv.at[0, j]).wait()
        g = core * heads + j
        block, logs = attend(q_all[1, :, cols(j)], j)
        o_out[j] = block

        @pl.when(n < EARLY)
        def _():
            sums_out[0, pl.ds(j, 1), :] = logs

        sums_out[1, pl.ds(j, 1), :] = logs

        @pl.when(n == EARLY - 1)
        def _():
            send_sums(0)

        @pl.when(n == heads - 1)
        def _():
            send_sums(1)

        held = jnp.where(z == far, pick(HOLD), 0)

        @pl.when(n >= held)
        def _():
            lax.fori_loop(jnp.where(n == held, 0, n), n + 1, send_part, 0)

        block, logs = attend(q_all[0, :, cols(j)], j)
        o_mine[j] = block
        sums_mine[pl.ds(j, 1), :] = logs
        pltpu.make_async_remote_copy(
            src_ref=o_mine.at[j, :, halves(other)], dst_ref=part_own.at[g],
            send_sem=mine_send, recv_sem=mine_recv.at[j],
            device_id=(inner, outer, other), device_id_type=MESH,
        ).start()
        part_own[g] = o_mine[j, :, halves(core)]

        return 0

    lax.fori_loop(0, heads, head_step, 0)
    sums_own[core] = sums_mine[:, halves(core)]
    swap = pltpu.make_async_remote_copy(
        src_ref=sums_mine.at[:, halves(other)], dst_ref=sums_own.at[core],
        send_sem=table_sem.at[0], recv_sem=table_sem.at[1],
        device_id=(inner, outer, other), device_id_type=MESH,
    )
    swap.start()
    swap.wait()

    def wait_sums(table):
        for c in range(2):
            pltpu.make_async_copy(sums_far.at[table, c], sums_far.at[table, c], sums_recv.at[table, c]).wait()

    wait_sums(0)
    lax.fori_loop(0, EARLY, lambda n, _: merge(n) or 0, 0)
    wait_sums(1)
    lax.fori_loop(EARLY, heads, lambda n, _: merge(n) or 0, 0)

    pltpu.make_async_copy(q_hbm, q_hbm, q_send).wait()

    @pl.when(handing)
    def _():
        pltpu.make_async_copy(q_all.at[2], q_all.at[2], hand_send).wait()

    pltpu.make_async_copy(k_hbm, k_hbm, kv_send.at[0]).wait()
    pltpu.make_async_copy(v_hbm, v_hbm, kv_send.at[1]).wait()
    pltpu.make_async_copy(o_out, o_out, far_send).wait()
    for table in range(2):
        pltpu.make_async_copy(sums_out.at[table], sums_out.at[table], sums_send.at[table]).wait()


    for own_y in range(along):
        for table, here in ((PASSES, (z > 0) & (z < far)), (PASSES_FAR, z == far), (PASSES_WRAP, wrap)):
            count = sum(own_y in ys for passes in table for kind, _, ys in passes if kind != "query")

            @pl.when((y == own_y) & here)
            def _():
                passed = kv_in.at[1, :, :, cols(0, count)]
                pltpu.make_async_copy(passed, passed, pass_send).wait()

    pltpu.make_async_copy(o_mine.at[:, :, halves(0)], o_mine.at[:, :, halves(0)], mine_send).wait()


def solution(mesh):
    n_inner, n_outer = mesh.shape["inner"], mesh.shape["outer"]

    def per_device(q, k, v):
        rows, width = q.shape
        heads = width // HD // 2
        both = 2 * rows
        dma = pltpu.SemaphoreType.DMA
        return pl.pallas_call(
            functools.partial(kernel, n_inner, n_outer, heads),
            out_shape=jax.ShapeDtypeStruct((rows, width), jnp.bfloat16),
            in_specs=[pl.BlockSpec(memory_space=pltpu.HBM)] * 3,
            out_specs=pl.BlockSpec(memory_space=pltpu.VMEM),
            scratch_shapes=[
                pltpu.VMEM((3, both, width // 2), jnp.bfloat16),
                pltpu.VMEM((2, both, width // 2), jnp.bfloat16),
                pltpu.VMEM((3, 2, both, width // 2), jnp.bfloat16),
                pltpu.VMEM((heads, HD, both), jnp.bfloat16),
                pltpu.VMEM((heads, HD, both), jnp.bfloat16),
                pltpu.VMEM((2 * heads, HD, rows), jnp.bfloat16),
                pltpu.VMEM((2 * heads, HD, rows), jnp.bfloat16),
                pltpu.VMEM((2, STATS, both), jnp.float32),
                pltpu.VMEM((STATS, both), jnp.float32),
                pltpu.VMEM((2, STATS, rows), jnp.float32),
                pltpu.VMEM((2, 2, STATS, rows), jnp.float32),
                pltpu.SemaphoreType.REGULAR, dma((3,)), dma((3,)), dma((3,)),
                dma, dma((3, heads)), dma, dma((2,)), dma((3, heads)), dma,
                dma, dma((2 * heads,)), dma, dma((heads,)), dma((2,)), dma((2, 2)), dma((2,)),
            ],
            compiler_params=pltpu.CompilerParams(
                collective_id=0, has_side_effects=True, vmem_limit_bytes=53 << 20
            ),
        )(q, k, v)

    spec = P(("inner", "outer", "head"), None)
    return jax.shard_map(per_device, mesh=mesh, in_specs=(spec,) * 3, out_specs=spec, check_vma=False)
```

```python
import functools
import math

import jax
import jax.numpy as jnp
from jax import lax
from jax.experimental import pallas as pl
from jax.experimental.pallas import tpu as pltpu
from jax.sharding import PartitionSpec as P

HD = 128
MESH = pl.DeviceIdType.MESH
LANE = 128
STATS = 16
EARLY = 8
BACK, BACK_WRAP = 8, 5
EVERY = (0, 1, 2, 3)
PASSES = (
    (("first", 8, EVERY),), (("first", 9, EVERY), ("second", 8, EVERY),), (("second", 9, EVERY),),
)
PASSES_FAR = (
    (("first", 8, EVERY), ("first", 9, EVERY), ("second", 8, (1, 2, 3)), ("second", 9, (1, 2, 3))),
    (("second", 8, (0,)),), (("second", 9, (0,)),),
)
PASSES_WRAP = (
    (("first", 8, EVERY), ("ring", 0, (0,)), ("first", 9, EVERY), ("query", 0, EVERY), ("ring", 1, (0,))),
    (("query", 1, EVERY), ("first", 6, (2,)), ("second", 8, (0, 1, 3)), ("ring", 2, (0,))),
    (("query", 2, EVERY), ("first", 7, (2,)), ("second", 9, (0, 1, 3)), ("ring", 3, (0,))),
    (("first", 5, (2,)), ("second", 6, (1,)), ("ring", 4, (0,))),
    (("second", 8, (2,)), ("second", 7, (1,))),
    (("second", 9, (2,)), ("second", 5, (1,))),
)
HOLD = (0, 0, 1, 0)
HANDED = (0, 3, 6, 10)
ORDER = (0, 1, 2, 3, 4, 8, 5, 9, 6, 7)
ORDER_WRAP = (0, 1, 2, 8, 3, 9, 6, 4, 7, 5)


def cols(at, count=1):
    return pl.ds(pl.multiple_of(at * HD, HD), count * HD)


def halves(at):
    return pl.ds(pl.multiple_of(at * LANE, LANE), LANE)


def kernel(
    n_inner, n_outer, heads,
    q_hbm, k_hbm, v_hbm, result,
    q_all, kv_own, kv_in, o_out, o_mine, part_own, part_far, sums_out, sums_mine, sums_own, sums_far,
    entered, own_sem, swap_send, swap_recv, q_send, q_recv, hand_send, kv_send, kv_recv, pass_send,
    far_send, far_recv, mine_send, mine_recv, sums_send, sums_recv, table_sem,
):
    inner, outer, core = lax.axis_index("inner"), lax.axis_index("outer"), lax.axis_index("head")
    rows = q_hbm.shape[0]
    other = 1 - core
    inner_up, inner_down = lax.rem(inner + 1, n_inner), lax.rem(inner + n_inner - 1, n_inner)
    outer_up, outer_down = lax.rem(outer + 1, n_outer), lax.rem(outer + n_outer - 1, n_outer)
    along = n_outer // 2
    side, y = outer // along, lax.rem(outer, along)
    flipped = (1 - side) * along + y
    z = lax.rem(inner, n_inner // 2)
    far = n_inner // 2 - 1
    wrap = z == 0
    mate = lax.rem(inner + n_inner // 2, n_inner)
    below, above = lax.rem(inner + far, n_inner), lax.rem(inner + n_inner - far, n_inner)
    by_mate = (y == along - 1) | (y == 1)
    handing, handed = wrap & by_mate, (z == far) & by_mate
    y_up, y_down = lax.rem(y + 1, along), lax.rem(y + along - 1, along)
    ring_up, ring_down = side * along + y_up, side * along + y_down
    cross_up, cross_down = (1 - side) * along + y_up, (1 - side) * along + y_down
    kv_far = kv_in.at[0]
    my_rows = pl.ds(pl.multiple_of(core * rows, rows), rows)

    own = []
    for at, (src, dst) in enumerate(((q_hbm, q_all.at[0]), (k_hbm, kv_own.at[0]), (v_hbm, kv_own.at[1]))):
        copy = pltpu.make_async_copy(src.at[:, cols(core * heads, heads)], dst.at[my_rows, :], own_sem.at[at])
        copy.start()
        own.append(copy)

    barrier = pltpu.get_barrier_semaphore()
    around = [(inner, outer, other)]
    for c in range(2):
        around += [(inner, at, c) for at in (outer_up, outer_down)]
    around += [(inner, at, core) for at in (flipped, cross_up, cross_down)]
    for device in around + [(inner_down, outer, c) for c in range(2)]:
        pl.semaphore_signal(barrier, inc=1, device_id=device, device_id_type=MESH)

    ends = (y == 0) | (y == along - 1)

    @pl.when(ends)
    def _():
        for c in range(2):
            device = (inner, jnp.where(y == 0, ring_down, ring_up), c)
            pl.semaphore_signal(barrier, inc=1, device_id=device, device_id_type=MESH)

    @pl.when(handing)
    def _():
        for at in (mate, below):
            for c in range(2):
                pl.semaphore_signal(barrier, inc=1, device_id=(at, outer, c), device_id_type=MESH)

    pl.semaphore_wait(barrier, len(around) + 2 + jnp.where(handing | handed, 2, 0) + jnp.where(ends, 2, 0))
    for c in range(2):
        device = (jnp.where(handed, above, inner_up), outer, c)
        pl.semaphore_signal(entered, inc=1, device_id=device, device_id_type=MESH)

    swaps = []
    for at, (src, dst) in enumerate(((q_hbm, q_all.at[0]), (k_hbm, kv_own.at[0]), (v_hbm, kv_own.at[1]))):
        copy = pltpu.make_async_remote_copy(
            src_ref=src.at[:, cols(other * heads, heads)], dst_ref=dst.at[my_rows, :],
            send_sem=swap_send.at[at], recv_sem=swap_recv.at[at],
            device_id=(inner, outer, other), device_id_type=MESH,
        )
        copy.start()
        swaps.append(copy)

    def send_head(n, _):
        late = jnp.where(n == heads - 1, BACK_WRAP, BACK_WRAP + 1 + lax.rem(n // 2 + 2, heads - BACK_WRAP - 1))
        last = (y == along - 1) & wrap
        j = jnp.where(last, jnp.where(lax.rem(n, 2) == 0, n // 2, late), jnp.where(n == 0, 0, jnp.where(n <= heads - BACK, n + BACK - 1, n + BACK - heads)))
        back = jnp.where(j >= BACK, 1, jnp.where(last & (j >= BACK_WRAP), 1, 0))
        by_ring = jnp.where(last & (back == 0), 1, 0)
        target = jnp.where(back == 1, ring_down, jnp.where(by_ring == 1, ring_up, outer_up))
        place = back + by_ring
        for at, src in enumerate((k_hbm, v_hbm)):
            for c in range(2):
                pltpu.make_async_remote_copy(
                    src_ref=src.at[:, cols(c * heads + j)], dst_ref=kv_in.at[place, at, my_rows, cols(j)],
                    send_sem=kv_send.at[at], recv_sem=kv_recv.at[place, j],
                    device_id=(inner, target, c), device_id_type=MESH,
                ).start()
        return 0

    q_place, q_target = jnp.where(handing, 2, 1), jnp.where(handing, mate, inner_down)

    def send_query(j, _):
        for c in range(2):
            pltpu.make_async_remote_copy(
                src_ref=q_hbm.at[:, cols(c * heads + j)], dst_ref=q_all.at[q_place, my_rows, cols(j)],
                send_sem=q_send, recv_sem=q_recv.at[q_place, j],
                device_id=(q_target, outer, c), device_id_type=MESH,
            ).start()
        return 0

    def hand_query(j, _):
        block = q_all.at[2, :, cols(j)]
        pltpu.make_async_copy(block, block, q_recv.at[2, j]).wait()
        pltpu.make_async_remote_copy(
            src_ref=block, dst_ref=q_all.at[1, :, cols(j)], send_sem=hand_send, recv_sem=q_recv.at[1, j],
            device_id=(below, outer, core), device_id_type=MESH,
        ).start()
        return 0

    @pl.when(handing)
    def _():
        lax.fori_loop(0, heads, send_query, 0)

    lax.fori_loop(0, heads, send_head, 0)

    @pl.when(z > 0)
    def _():
        pl.semaphore_wait(entered, 2)
        lax.fori_loop(0, heads, send_query, 0)

    for copy in own:
        copy.wait()
    for copy in swaps:
        copy.wait()

    factor = math.log2(math.e) / math.sqrt(HD)

    def attend(q, j):
        keys = (kv_own[0, :, cols(j)], kv_in[0, 0, :, cols(j)])
        values = (kv_own[1, :, cols(j)], kv_in[0, 1, :, cols(j)])
        scores = [
            lax.dot_general(k, q, (((1,), (1,)), ((), ())), preferred_element_type=jnp.float32) for k in keys
        ]
        top = jnp.max(jnp.maximum(scores[0], scores[1]), axis=0, keepdims=True)
        weights = [jnp.exp2((s - top) * factor) for s in scores]
        total = jnp.sum(weights[0] + weights[1], axis=0, keepdims=True)
        summed = sum(
            lax.dot_general(
                v, w.astype(jnp.bfloat16), (((0,), (0,)), ((), ())), preferred_element_type=jnp.float32
            )
            for v, w in zip(values, weights)
        )
        return (summed * (1.0 / total)).astype(jnp.bfloat16), top * factor + jnp.log2(total)

    def merge(n):
        j = sent_at(n)
        for c in range(2):
            g = c * heads + j
            pltpu.make_async_copy(part_far.at[g], part_far.at[g], far_recv.at[g]).wait()

        pltpu.make_async_copy(
            part_own.at[other * heads + j], part_own.at[other * heads + j], mine_recv.at[j]
        ).wait()
        table = jnp.where(n < EARLY, 0, 1)
        for c in range(2):
            g = c * heads + j
            log_own, log_far = sums_own[c, pl.ds(j, 1), :], sums_far[table, c, pl.ds(j, 1), :]
            share_own = 1.0 / (1.0 + jnp.exp2(log_far - log_own))
            share_far = 1.0 / (1.0 + jnp.exp2(log_own - log_far))
            mixed = part_own[g].astype(jnp.float32) * share_own + part_far[g].astype(jnp.float32) * share_far
            result[:, cols(g)] = mixed.T.astype(jnp.bfloat16)

    def pass_on(kind, j):
        source, place, target = {
            "first": (1, 2, jnp.where((y == 2) & (wrap if j % 2 else z < far), cross_down, ring_down)),
            "second": (2, 0, jnp.where((y == 1) & (z > 0 if j % 2 else z == far), cross_down, ring_down)),
            "ring": (1, 0, flipped),
        }[kind]
        block = kv_in.at[source, :, :, cols(j)]
        pltpu.make_async_copy(block, block, kv_recv.at[source, j]).wait()
        pltpu.make_async_remote_copy(
            src_ref=block, dst_ref=kv_in.at[place, :, :, cols(j)], send_sem=pass_send, recv_sem=kv_recv.at[place, j],
            device_id=(inner, target, core), device_id_type=MESH,
        ).start()

    def listed(order, n):
        head = order[0]
        for at, j in enumerate(order):
            head = jnp.where(n == at, j, head)
        return head

    def pick(by_y):
        return listed(by_y, y)

    def head_at(n):
        return jnp.where(wrap, jnp.where(y == 0, listed(ORDER_WRAP, n), n), listed(ORDER, n))

    def sent_at(n):
        return jnp.where(z == 1, jnp.where(y == 0, listed(ORDER_WRAP, n), n), listed(ORDER, n))

    def send_sums(table):
        for c in range(2):
            pltpu.make_async_remote_copy(
                src_ref=sums_out.at[table, :, halves(c)], dst_ref=sums_far.at[table, core],
                send_sem=sums_send.at[table], recv_sem=sums_recv.at[table, core],
                device_id=(inner_up, outer, c), device_id_type=MESH,
            ).start()

    def run_passes(passes):
        for kind, which, ys in passes:

            @pl.when(functools.reduce(jnp.logical_or, [y == own_y for own_y in ys]))
            def _():
                if kind != "query":
                    pass_on(kind, which)
                    return

                if which == 0:
                    pl.semaphore_wait(entered, 2)

                @pl.when(jnp.logical_not(handing))
                def _():
                    lax.fori_loop(HANDED[which], HANDED[which + 1], send_query, 0)

                @pl.when(handing)
                def _():
                    lax.fori_loop(HANDED[which], HANDED[which + 1], hand_query, 0)

    def send_part(n, _):
        j = head_at(n)
        for c in range(2):
            pltpu.make_async_remote_copy(
                src_ref=o_out.at[j, :, halves(c)], dst_ref=part_far.at[core * heads + j],
                send_sem=far_send, recv_sem=far_recv.at[core * heads + j],
                device_id=(inner_up, outer, c), device_id_type=MESH,
            ).start()
        return 0

    def head_step(n, _):
        for table, here in ((PASSES, (z > 0) & (z < far)), (PASSES_FAR, z == far), (PASSES_WRAP, wrap)):
            for at, passes in enumerate(table):

                @pl.when((n == at) & here)
                def _():
                    run_passes(passes)

        j = head_at(n)
        pltpu.make_async_copy(q_all.at[1, :, cols(j)], q_all.at[1, :, cols(j)], q_recv.at[1, j]).wait()
        pltpu.make_async_copy(kv_far.at[:, :, cols(j)], kv_far.at[:, :, cols(j)], kv_recv.at[0, j]).wait()
        g = core * heads + j
        block, logs = attend(q_all[1, :, cols(j)], j)
        o_out[j] = block

        @pl.when(n < EARLY)
        def _():
            sums_out[0, pl.ds(j, 1), :] = logs

        sums_out[1, pl.ds(j, 1), :] = logs

        @pl.when(n == EARLY - 1)
        def _():
            send_sums(0)

        @pl.when(n == heads - 1)
        def _():
            send_sums(1)

        held = jnp.where(z == far, pick(HOLD), 0)

        @pl.when(n >= held)
        def _():
            lax.fori_loop(jnp.where(n == held, 0, n), n + 1, send_part, 0)

        block, logs = attend(q_all[0, :, cols(j)], j)
        o_mine[j] = block
        sums_mine[pl.ds(j, 1), :] = logs
        pltpu.make_async_remote_copy(
            src_ref=o_mine.at[j, :, halves(other)], dst_ref=part_own.at[g],
            send_sem=mine_send, recv_sem=mine_recv.at[j],
            device_id=(inner, outer, other), device_id_type=MESH,
        ).start()
        part_own[g] = o_mine[j, :, halves(core)]

        return 0

    lax.fori_loop(0, heads, head_step, 0)
    sums_own[core] = sums_mine[:, halves(core)]
    swap = pltpu.make_async_remote_copy(
        src_ref=sums_mine.at[:, halves(other)], dst_ref=sums_own.at[core],
        send_sem=table_sem.at[0], recv_sem=table_sem.at[1],
        device_id=(inner, outer, other), device_id_type=MESH,
    )
    swap.start()
    swap.wait()

    def wait_sums(table):
        for c in range(2):
            pltpu.make_async_copy(sums_far.at[table, c], sums_far.at[table, c], sums_recv.at[table, c]).wait()

    wait_sums(0)
    lax.fori_loop(0, EARLY, lambda n, _: merge(n) or 0, 0)
    wait_sums(1)
    lax.fori_loop(EARLY, heads, lambda n, _: merge(n) or 0, 0)

    pltpu.make_async_copy(q_hbm, q_hbm, q_send).wait()

    @pl.when(handing)
    def _():
        pltpu.make_async_copy(q_all.at[2], q_all.at[2], hand_send).wait()

    pltpu.make_async_copy(k_hbm, k_hbm, kv_send.at[0]).wait()
    pltpu.make_async_copy(v_hbm, v_hbm, kv_send.at[1]).wait()
    pltpu.make_async_copy(o_out, o_out, far_send).wait()
    for table in range(2):
        pltpu.make_async_copy(sums_out.at[table], sums_out.at[table], sums_send.at[table]).wait()


    for own_y in range(along):
        for table, here in ((PASSES, (z > 0) & (z < far)), (PASSES_FAR, z == far), (PASSES_WRAP, wrap)):
            count = sum(own_y in ys for passes in table for kind, _, ys in passes if kind != "query")

            @pl.when((y == own_y) & here)
            def _():
                passed = kv_in.at[1, :, :, cols(0, count)]
                pltpu.make_async_copy(passed, passed, pass_send).wait()

    pltpu.make_async_copy(o_mine.at[:, :, halves(0)], o_mine.at[:, :, halves(0)], mine_send).wait()


def solution(mesh):
    n_inner, n_outer = mesh.shape["inner"], mesh.shape["outer"]

    def per_device(q, k, v):
        rows, width = q.shape
        heads = width // HD // 2
        both = 2 * rows
        dma = pltpu.SemaphoreType.DMA
        return pl.pallas_call(
            functools.partial(kernel, n_inner, n_outer, heads),
            out_shape=jax.ShapeDtypeStruct((rows, width), jnp.bfloat16),
            in_specs=[pl.BlockSpec(memory_space=pltpu.HBM)] * 3,
            out_specs=pl.BlockSpec(memory_space=pltpu.VMEM),
            scratch_shapes=[
                pltpu.VMEM((3, both, width // 2), jnp.bfloat16),
                pltpu.VMEM((2, both, width // 2), jnp.bfloat16),
                pltpu.VMEM((3, 2, both, width // 2), jnp.bfloat16),
                pltpu.VMEM((heads, HD, both), jnp.bfloat16),
                pltpu.VMEM((heads, HD, both), jnp.bfloat16),
                pltpu.VMEM((2 * heads, HD, rows), jnp.bfloat16),
                pltpu.VMEM((2 * heads, HD, rows), jnp.bfloat16),
                pltpu.VMEM((2, STATS, both), jnp.float32),
                pltpu.VMEM((STATS, both), jnp.float32),
                pltpu.VMEM((2, STATS, rows), jnp.float32),
                pltpu.VMEM((2, 2, STATS, rows), jnp.float32),
                pltpu.SemaphoreType.REGULAR, dma((3,)), dma((3,)), dma((3,)),
                dma, dma((3, heads)), dma, dma((2,)), dma((3, heads)), dma,
                dma, dma((2 * heads,)), dma, dma((heads,)), dma((2,)), dma((2, 2)), dma((2,)),
            ],
            compiler_params=pltpu.CompilerParams(
                collective_id=0, has_side_effects=True, vmem_limit_bytes=53 << 20
            ),
        )(q, k, v)

    spec = P(("inner", "outer", "head"), None)
    return jax.shard_map(per_device, mesh=mesh, in_specs=(spec,) * 3, out_specs=spec, check_vma=False)
```

```python
import functools
import math

import jax
import jax.numpy as jnp
from jax import lax
from jax.experimental import pallas as pl
from jax.experimental.pallas import tpu as pltpu
from jax.sharding import PartitionSpec as P

HD = 128
MESH = pl.DeviceIdType.MESH
LANE = 128
STATS = 16
EARLY = 9
BACK, BACK_WRAP = 8, 5
EVERY = (0, 1, 2, 3)
PASSES = (
    (("first", 8, EVERY),), (("first", 9, EVERY), ("second", 8, EVERY),), (("second", 9, EVERY),),
)
PASSES_FAR = (
    (("first", 8, EVERY), ("first", 9, EVERY), ("second", 8, (1, 2, 3)), ("second", 9, (1, 2, 3))),
    (("second", 8, (0,)),), (("second", 9, (0,)),),
)
PASSES_WRAP = (
    (("first", 8, EVERY), ("ring", 0, (0,)), ("first", 9, EVERY), ("query", 0, EVERY), ("ring", 1, (0,))),
    (("query", 1, EVERY), ("first", 6, (2,)), ("second", 8, (0, 1, 3)), ("ring", 2, (0,))),
    (("query", 2, EVERY), ("first", 7, (2,)), ("second", 9, (0, 1, 3)), ("ring", 3, (0,))),
    (("first", 5, (2,)), ("second", 6, (1,)), ("ring", 4, (0,))),
    (("second", 8, (2,)), ("second", 7, (1,))),
    (("second", 9, (2,)), ("second", 5, (1,))),
)
HOLD = (0, 0, 1, 0)
HANDED = (0, 3, 6, 10)
ORDER = (0, 1, 2, 3, 4, 8, 5, 9, 6, 7)
ORDER_WRAP = (0, 1, 2, 8, 3, 9, 6, 4, 7, 5)


def cols(at, count=1):
    return pl.ds(pl.multiple_of(at * HD, HD), count * HD)


def halves(at):
    return pl.ds(pl.multiple_of(at * LANE, LANE), LANE)


def kernel(
    n_inner, n_outer, heads,
    q_hbm, k_hbm, v_hbm, result,
    q_all, kv_own, kv_in, o_out, o_mine, part_own, part_far, sums_out, sums_mine, sums_own, sums_far,
    entered, own_sem, swap_send, swap_recv, q_send, q_recv, hand_send, kv_send, kv_recv, pass_send,
    far_send, far_recv, mine_send, mine_recv, sums_send, sums_recv, table_sem,
):
    inner, outer, core = lax.axis_index("inner"), lax.axis_index("outer"), lax.axis_index("head")
    rows = q_hbm.shape[0]
    other = 1 - core
    inner_up, inner_down = lax.rem(inner + 1, n_inner), lax.rem(inner + n_inner - 1, n_inner)
    outer_up, outer_down = lax.rem(outer + 1, n_outer), lax.rem(outer + n_outer - 1, n_outer)
    along = n_outer // 2
    side, y = outer // along, lax.rem(outer, along)
    flipped = (1 - side) * along + y
    z = lax.rem(inner, n_inner // 2)
    far = n_inner // 2 - 1
    wrap = z == 0
    mate = lax.rem(inner + n_inner // 2, n_inner)
    below, above = lax.rem(inner + far, n_inner), lax.rem(inner + n_inner - far, n_inner)
    by_mate = (y == along - 1) | (y == 1)
    handing, handed = wrap & by_mate, (z == far) & by_mate
    y_up, y_down = lax.rem(y + 1, along), lax.rem(y + along - 1, along)
    ring_up, ring_down = side * along + y_up, side * along + y_down
    cross_up, cross_down = (1 - side) * along + y_up, (1 - side) * along + y_down
    kv_far = kv_in.at[0]
    my_rows = pl.ds(pl.multiple_of(core * rows, rows), rows)

    own = []
    for at, (src, dst) in enumerate(((q_hbm, q_all.at[0]), (k_hbm, kv_own.at[0]), (v_hbm, kv_own.at[1]))):
        copy = pltpu.make_async_copy(src.at[:, cols(core * heads, heads)], dst.at[my_rows, :], own_sem.at[at])
        copy.start()
        own.append(copy)

    barrier = pltpu.get_barrier_semaphore()
    around = [(inner, outer, other)]
    for c in range(2):
        around += [(inner, at, c) for at in (outer_up, outer_down, ring_up, ring_down)]
    around += [(inner, at, core) for at in (flipped, cross_up, cross_down)]
    for device in around + [(inner_down, outer, c) for c in range(2)]:
        pl.semaphore_signal(barrier, inc=1, device_id=device, device_id_type=MESH)

    @pl.when(handing)
    def _():
        for at in (mate, below):
            for c in range(2):
                pl.semaphore_signal(barrier, inc=1, device_id=(at, outer, c), device_id_type=MESH)

    pl.semaphore_wait(barrier, len(around) + 2 + jnp.where(handing | handed, 2, 0))
    for c in range(2):
        device = (jnp.where(handed, above, inner_up), outer, c)
        pl.semaphore_signal(entered, inc=1, device_id=device, device_id_type=MESH)

    swaps = []
    for at, (src, dst) in enumerate(((q_hbm, q_all.at[0]), (k_hbm, kv_own.at[0]), (v_hbm, kv_own.at[1]))):
        copy = pltpu.make_async_remote_copy(
            src_ref=src.at[:, cols(other * heads, heads)], dst_ref=dst.at[my_rows, :],
            send_sem=swap_send.at[at], recv_sem=swap_recv.at[at],
            device_id=(inner, outer, other), device_id_type=MESH,
        )
        copy.start()
        swaps.append(copy)

    def send_head(n, _):
        late = jnp.where(n == heads - 1, BACK_WRAP, BACK_WRAP + 1 + lax.rem(n // 2 + 2, heads - BACK_WRAP - 1))
        last = (y == along - 1) & wrap
        j = jnp.where(last, jnp.where(lax.rem(n, 2) == 0, n // 2, late), lax.rem(n + BACK, heads))
        back = jnp.where(j >= BACK, 1, jnp.where(last & (j >= BACK_WRAP), 1, 0))
        by_ring = jnp.where(last & (back == 0), 1, 0)
        target = jnp.where(back == 1, ring_down, jnp.where(by_ring == 1, ring_up, outer_up))
        place = back + by_ring
        for at, src in enumerate((k_hbm, v_hbm)):
            for c in range(2):
                pltpu.make_async_remote_copy(
                    src_ref=src.at[:, cols(c * heads + j)], dst_ref=kv_in.at[place, at, my_rows, cols(j)],
                    send_sem=kv_send.at[at], recv_sem=kv_recv.at[place, j],
                    device_id=(inner, target, c), device_id_type=MESH,
                ).start()
        return 0

    q_place, q_target = jnp.where(handing, 2, 1), jnp.where(handing, mate, inner_down)

    def send_query(j, _):
        for c in range(2):
            pltpu.make_async_remote_copy(
                src_ref=q_hbm.at[:, cols(c * heads + j)], dst_ref=q_all.at[q_place, my_rows, cols(j)],
                send_sem=q_send, recv_sem=q_recv.at[q_place, j],
                device_id=(q_target, outer, c), device_id_type=MESH,
            ).start()
        return 0

    def hand_query(j, _):
        block = q_all.at[2, :, cols(j)]
        pltpu.make_async_copy(block, block, q_recv.at[2, j]).wait()
        pltpu.make_async_remote_copy(
            src_ref=block, dst_ref=q_all.at[1, :, cols(j)], send_sem=hand_send, recv_sem=q_recv.at[1, j],
            device_id=(below, outer, core), device_id_type=MESH,
        ).start()
        return 0

    @pl.when(handing)
    def _():
        lax.fori_loop(0, heads, send_query, 0)

    lax.fori_loop(0, heads, send_head, 0)

    @pl.when(z > 0)
    def _():
        pl.semaphore_wait(entered, 2)
        lax.fori_loop(0, heads, send_query, 0)

    for copy in own:
        copy.wait()
    for copy in swaps:
        copy.wait()

    factor = math.log2(math.e) / math.sqrt(HD)

    def attend(q, j):
        keys = (kv_own[0, :, cols(j)], kv_in[0, 0, :, cols(j)])
        values = (kv_own[1, :, cols(j)], kv_in[0, 1, :, cols(j)])
        scores = [
            lax.dot_general(k, q, (((1,), (1,)), ((), ())), preferred_element_type=jnp.float32) for k in keys
        ]
        top = jnp.max(jnp.maximum(scores[0], scores[1]), axis=0, keepdims=True)
        weights = [jnp.exp2((s - top) * factor) for s in scores]
        total = jnp.sum(weights[0] + weights[1], axis=0, keepdims=True)
        summed = sum(
            lax.dot_general(
                v, w.astype(jnp.bfloat16), (((0,), (0,)), ((), ())), preferred_element_type=jnp.float32
            )
            for v, w in zip(values, weights)
        )
        return (summed * (1.0 / total)).astype(jnp.bfloat16), top * factor + jnp.log2(total)

    def merge(n):
        j = sent_at(n)
        for c in range(2):
            g = c * heads + j
            pltpu.make_async_copy(part_far.at[g], part_far.at[g], far_recv.at[g]).wait()

        pltpu.make_async_copy(
            part_own.at[other * heads + j], part_own.at[other * heads + j], mine_recv.at[j]
        ).wait()
        table = jnp.where(n < EARLY, 0, 1)
        for c in range(2):
            g = c * heads + j
            log_own, log_far = sums_own[c, pl.ds(j, 1), :], sums_far[table, c, pl.ds(j, 1), :]
            share_own = 1.0 / (1.0 + jnp.exp2(log_far - log_own))
            share_far = 1.0 / (1.0 + jnp.exp2(log_own - log_far))
            mixed = part_own[g].astype(jnp.float32) * share_own + part_far[g].astype(jnp.float32) * share_far
            result[:, cols(g)] = mixed.T.astype(jnp.bfloat16)

    def pass_on(kind, j):
        source, place, target = {
            "first": (1, 2, jnp.where((y == 2) & (wrap if j % 2 else z < far), cross_down, ring_down)),
            "second": (2, 0, jnp.where((y == 1) & (z > 0 if j % 2 else z == far), cross_down, ring_down)),
            "ring": (1, 0, flipped),
        }[kind]
        block = kv_in.at[source, :, :, cols(j)]
        pltpu.make_async_copy(block, block, kv_recv.at[source, j]).wait()
        pltpu.make_async_remote_copy(
            src_ref=block, dst_ref=kv_in.at[place, :, :, cols(j)], send_sem=pass_send, recv_sem=kv_recv.at[place, j],
            device_id=(inner, target, core), device_id_type=MESH,
        ).start()

    def listed(order, n):
        head = order[0]
        for at, j in enumerate(order):
            head = jnp.where(n == at, j, head)
        return head

    def pick(by_y):
        return listed(by_y, y)

    def head_at(n):
        return jnp.where(wrap, jnp.where(y == 0, listed(ORDER_WRAP, n), n), listed(ORDER, n))

    def sent_at(n):
        return jnp.where(z == 1, jnp.where(y == 0, listed(ORDER_WRAP, n), n), listed(ORDER, n))

    def send_sums(table):
        for c in range(2):
            pltpu.make_async_remote_copy(
                src_ref=sums_out.at[table, :, halves(c)], dst_ref=sums_far.at[table, core],
                send_sem=sums_send.at[table], recv_sem=sums_recv.at[table, core],
                device_id=(inner_up, outer, c), device_id_type=MESH,
            ).start()

    def run_passes(passes):
        for kind, which, ys in passes:

            @pl.when(functools.reduce(jnp.logical_or, [y == own_y for own_y in ys]))
            def _():
                if kind != "query":
                    pass_on(kind, which)
                    return

                if which == 0:
                    pl.semaphore_wait(entered, 2)

                @pl.when(jnp.logical_not(handing))
                def _():
                    lax.fori_loop(HANDED[which], HANDED[which + 1], send_query, 0)

                @pl.when(handing)
                def _():
                    lax.fori_loop(HANDED[which], HANDED[which + 1], hand_query, 0)

    def send_part(n, _):
        j = head_at(n)
        for c in range(2):
            pltpu.make_async_remote_copy(
                src_ref=o_out.at[j, :, halves(c)], dst_ref=part_far.at[core * heads + j],
                send_sem=far_send, recv_sem=far_recv.at[core * heads + j],
                device_id=(inner_up, outer, c), device_id_type=MESH,
            ).start()
        return 0

    def head_step(n, _):
        for table, here in ((PASSES, (z > 0) & (z < far)), (PASSES_FAR, z == far), (PASSES_WRAP, wrap)):
            for at, passes in enumerate(table):

                @pl.when((n == at) & here)
                def _():
                    run_passes(passes)

        j = head_at(n)
        pltpu.make_async_copy(q_all.at[1, :, cols(j)], q_all.at[1, :, cols(j)], q_recv.at[1, j]).wait()
        pltpu.make_async_copy(kv_far.at[:, :, cols(j)], kv_far.at[:, :, cols(j)], kv_recv.at[0, j]).wait()
        g = core * heads + j
        block, logs = attend(q_all[1, :, cols(j)], j)
        o_out[j] = block

        @pl.when(n < EARLY)
        def _():
            sums_out[0, pl.ds(j, 1), :] = logs

        sums_out[1, pl.ds(j, 1), :] = logs

        @pl.when(n == EARLY - 1)
        def _():
            send_sums(0)

        @pl.when(n == heads - 1)
        def _():
            send_sums(1)

        held = jnp.where(z == far, pick(HOLD), 0)

        @pl.when(n >= held)
        def _():
            lax.fori_loop(jnp.where(n == held, 0, n), n + 1, send_part, 0)

        block, logs = attend(q_all[0, :, cols(j)], j)
        o_mine[j] = block
        sums_mine[pl.ds(j, 1), :] = logs
        pltpu.make_async_remote_copy(
            src_ref=o_mine.at[j, :, halves(other)], dst_ref=part_own.at[g],
            send_sem=mine_send, recv_sem=mine_recv.at[j],
            device_id=(inner, outer, other), device_id_type=MESH,
        ).start()
        part_own[g] = o_mine[j, :, halves(core)]

        return 0

    lax.fori_loop(0, heads, head_step, 0)
    sums_own[core] = sums_mine[:, halves(core)]
    swap = pltpu.make_async_remote_copy(
        src_ref=sums_mine.at[:, halves(other)], dst_ref=sums_own.at[core],
        send_sem=table_sem.at[0], recv_sem=table_sem.at[1],
        device_id=(inner, outer, other), device_id_type=MESH,
    )
    swap.start()
    swap.wait()

    def wait_sums(table):
        for c in range(2):
            pltpu.make_async_copy(sums_far.at[table, c], sums_far.at[table, c], sums_recv.at[table, c]).wait()

    wait_sums(0)
    lax.fori_loop(0, EARLY, lambda n, _: merge(n) or 0, 0)
    wait_sums(1)
    lax.fori_loop(EARLY, heads, lambda n, _: merge(n) or 0, 0)

    pltpu.make_async_copy(q_hbm, q_hbm, q_send).wait()

    @pl.when(handing)
    def _():
        pltpu.make_async_copy(q_all.at[2], q_all.at[2], hand_send).wait()

    pltpu.make_async_copy(k_hbm, k_hbm, kv_send.at[0]).wait()
    pltpu.make_async_copy(v_hbm, v_hbm, kv_send.at[1]).wait()
    pltpu.make_async_copy(o_out, o_out, far_send).wait()
    for table in range(2):
        pltpu.make_async_copy(sums_out.at[table], sums_out.at[table], sums_send.at[table]).wait()


    for own_y in range(along):
        for table, here in ((PASSES, (z > 0) & (z < far)), (PASSES_FAR, z == far), (PASSES_WRAP, wrap)):
            count = sum(own_y in ys for passes in table for kind, _, ys in passes if kind != "query")

            @pl.when((y == own_y) & here)
            def _():
                passed = kv_in.at[1, :, :, cols(0, count)]
                pltpu.make_async_copy(passed, passed, pass_send).wait()

    pltpu.make_async_copy(o_mine.at[:, :, halves(0)], o_mine.at[:, :, halves(0)], mine_send).wait()


def solution(mesh):
    n_inner, n_outer = mesh.shape["inner"], mesh.shape["outer"]

    def per_device(q, k, v):
        rows, width = q.shape
        heads = width // HD // 2
        both = 2 * rows
        dma = pltpu.SemaphoreType.DMA
        return pl.pallas_call(
            functools.partial(kernel, n_inner, n_outer, heads),
            out_shape=jax.ShapeDtypeStruct((rows, width), jnp.bfloat16),
            in_specs=[pl.BlockSpec(memory_space=pltpu.HBM)] * 3,
            out_specs=pl.BlockSpec(memory_space=pltpu.VMEM),
            scratch_shapes=[
                pltpu.VMEM((3, both, width // 2), jnp.bfloat16),
                pltpu.VMEM((2, both, width // 2), jnp.bfloat16),
                pltpu.VMEM((3, 2, both, width // 2), jnp.bfloat16),
                pltpu.VMEM((heads, HD, both), jnp.bfloat16),
                pltpu.VMEM((heads, HD, both), jnp.bfloat16),
                pltpu.VMEM((2 * heads, HD, rows), jnp.bfloat16),
                pltpu.VMEM((2 * heads, HD, rows), jnp.bfloat16),
                pltpu.VMEM((2, STATS, both), jnp.float32),
                pltpu.VMEM((STATS, both), jnp.float32),
                pltpu.VMEM((2, STATS, rows), jnp.float32),
                pltpu.VMEM((2, 2, STATS, rows), jnp.float32),
                pltpu.SemaphoreType.REGULAR, dma((3,)), dma((3,)), dma((3,)),
                dma, dma((3, heads)), dma, dma((2,)), dma((3, heads)), dma,
                dma, dma((2 * heads,)), dma, dma((heads,)), dma((2,)), dma((2, 2)), dma((2,)),
            ],
            compiler_params=pltpu.CompilerParams(
                collective_id=0, has_side_effects=True, vmem_limit_bytes=53 << 20
            ),
        )(q, k, v)

    spec = P(("inner", "outer", "head"), None)
    return jax.shard_map(per_device, mesh=mesh, in_specs=(spec,) * 3, out_specs=spec, check_vma=False)
```
